256 devices in a mesh: rows: 64 (over y, z, core), cell: 4 (over x).
Axes of the slice: x: 4, y: 4, z: 8, core: 2. Of those that a mesh axis runs over, the one named last changes fastest.
Arguments:
- covariates: bfloat16 [1048576, 128], P('rows'), may hold values from -6 to 6, as said below
- outcomes: float32 [8, 1048576], P(None, 'rows'), may hold values from -60 to 60
- multipliers: bfloat16 [1048576, 512], P('rows', 'cell'), may hold values from -5 to 5
- cohorts: int32 [8192], P('rows'), may hold values from 3 to 8, as said below
- cells: int32 [4, 2], P('cell'), may hold values from 3 to 7, as said below
Outputs:
- influence: float32 [4, 1048576], P('cell', 'rows')
- bootstrap: float32 [4, 512], P(None, 'cell')
The draws below stay inside these ranges and needn't reach their ends.
Inputs may be any that keep to these rules, and one draw needn't show every extreme that they name: `cohorts`: blocks are in non-decreasing order of cohort, and every cohort from 3 to 8 holds at least one block. `cells`: each cell's period is at least its group. `covariates`: column 0 is 1 for every worker.
All inputs are finite; a program needn't handle non-finite values.
Results may differ from the reference program's by a relative error of at most 0.006.
The reference program's roundings to bfloat16 on the way (of `scaled`) count: a program that leaves them out, or rounds other values in their place, can miss the bound.
Values may be sent and summed in bfloat16 or wider, within the bound.
No kernel may reach another device: no remote copies, remote signals or barrier semaphores. Data moves between devices by JAX's collectives and lax.ppermute only.
A program may use at most 128 MiB of HBM per device.

```python
import math
import jax
import jax.numpy as jnp
from jax import lax

P_SIZE = 128
BLOCK = 128
PERIODS = 8
NEWTON = 3
DRAWS = 512
CELLS = 4
ROWS = 1048576
NBLOCKS = 8192


def cohort_law(key):
    table = jnp.array([3, 3, 3, 3, 3, 4, 4, 4, 5, 5, 6, 6, 7, 7, 8, 8], jnp.int32)
    picks = jax.random.randint(jax.random.fold_in(key, 11), (NBLOCKS,), 0, 16)
    values = jnp.take(table, picks).astype(jnp.int32)
    places = jnp.arange(NBLOCKS).astype(jnp.int32)
    values = jnp.where(places < PERIODS - 2, places + 3, values)
    return jnp.sort(values).astype(jnp.int32)


def cohort_shift(key):
    cohort_rows = jnp.repeat(cohort_law(key), BLOCK)
    means = jnp.clip(jax.random.normal(jax.random.fold_in(key, 23), (PERIODS + 1, P_SIZE), jnp.float32), -2.5, 2.5)
    means = means * (1.5 / math.sqrt(P_SIZE - 1))
    column_ids = jnp.arange(P_SIZE)
    means = jnp.where(column_ids[None, :] == 0, 0.0, means)
    return jnp.take(means, cohort_rows, axis=0)


def leading_columns(key):
    shift = cohort_shift(key)[:, :8]
    leading = jnp.clip(jax.random.normal(jax.random.fold_in(key, 21), (ROWS, 8), jnp.float32), -5.5, 5.5)
    leading = leading + shift
    column_ids = jnp.arange(8)
    leading = jnp.where(column_ids[None, :] == 0, 1.0, leading)
    return jnp.clip(leading, -6.0, 6.0)


def other_columns(key):
    shift = cohort_shift(key)[:, 8:]
    noise = jnp.clip(jax.random.normal(jax.random.fold_in(key, 22), (ROWS, P_SIZE - 8), jnp.float32), -5.5, 5.5)
    return jnp.clip(noise + shift, -6.0, 6.0)


def draw_covariates(key, part):
    return jnp.concatenate([leading_columns(key), other_columns(key)], axis=1).astype(jnp.bfloat16)


def draw_outcomes(key, part):
    leading = leading_columns(key)
    slopes = 0.5 * jnp.clip(jax.random.normal(jax.random.fold_in(key, 31), (PERIODS, 8), jnp.float32), -2.5, 2.5)
    earnings = 0.7 * jnp.clip(jax.random.normal(jax.random.fold_in(key, 32), (PERIODS, ROWS), jnp.float32), -5.0, 5.0)
    for column in range(8):
        earnings = earnings + slopes[:, column][:, None] * leading[:, column][None, :]
    return earnings.astype(jnp.float32)


def draw_cohorts(key, part):
    return cohort_law(key)


def draw_cells(key, part):
    first_key, second_key = jax.random.split(jax.random.fold_in(key, 7))
    treat_group = jax.random.randint(first_key, (CELLS,), 3, PERIODS)
    offset = jax.random.randint(second_key, (CELLS,), 0, PERIODS - treat_group)
    return jnp.stack([treat_group, treat_group + offset], axis=1).astype(jnp.int32)


def shard_levels(own_key, extent, pieces, smallest, high):
    level = 1.0
    for axis_at, parts in pieces:
        heights = jax.random.uniform(jax.random.fold_in(jax.random.fold_in(own_key, 6), axis_at), (parts,), jnp.float32, smallest / len(pieces), high / len(pieces))
        level = level * jnp.repeat(jnp.exp(heights), extent[axis_at] // parts).reshape((-1,) + (1,) * (len(extent) - 1 - axis_at))
    return level


def bell_draw(own_key, extent, deviation, bound, cuts=(), held_as=jnp.bfloat16):
    drawn = jax.random.normal(own_key, extent, jnp.float32) * deviation
    if len(cuts) > 0:
        drawn = shard_levels(own_key, extent, cuts, -0.22, 0.18) * drawn
    return jnp.clip(drawn, min=-bound, max=bound).astype(held_as)


def setup_inputs(seed: int = 0) -> dict:
    streams_of = jax.random.split(jax.random.key(seed), 6)
    return {
        "covariates": draw_covariates(jax.random.fold_in(streams_of[5], 71), 0),
        "outcomes": draw_outcomes(jax.random.fold_in(streams_of[5], 71), 0),
        "multipliers": bell_draw(streams_of[2], (ROWS, DRAWS), 1.0, 5.0, ((0, 64), (1, 4))),
        "cohorts": draw_cohorts(jax.random.fold_in(streams_of[5], 71), 0),
        "cells": draw_cells(jax.random.fold_in(streams_of[5], 71), 0),
    }


def cross_rows(left, right):
    return lax.dot_general(left.astype(jnp.float32), right.astype(jnp.float32), (((0,), (0,)), ((), ())), preferred_element_type=jnp.float32)

def newton_solve(matrix, vector):
    factor = jnp.linalg.cholesky(matrix)
    return jax.scipy.linalg.cho_solve((factor, True), vector.reshape(-1, 1)).reshape(-1)

def reference(covariates, outcomes, multipliers, cohorts, cells):
    total_rows = covariates.shape[0]
    block_rows = total_rows // cohorts.shape[0]
    cohort_rows = jnp.repeat(cohorts, block_rows)
    period_ids = jnp.arange(outcomes.shape[0])
    results = []
    draws_out = []
    for which in range(cells.shape[0]):
        treat_group = cells[which, 0]
        period = cells[which, 1]
        treated = (cohort_rows == treat_group).astype(jnp.float32)
        control = (cohort_rows > period).astype(jnp.float32)
        eligible = treated + control
        period_select = (period_ids == period).astype(jnp.float32) - (period_ids == treat_group - 1).astype(jnp.float32)
        change = jnp.dot(period_select, outcomes, precision=lax.Precision.HIGHEST)
        ctrl_x = control.astype(jnp.bfloat16)[:, None] * covariates
        ctrl_gram = cross_rows(ctrl_x, covariates)
        ctrl_moment = cross_rows((control * change).astype(jnp.bfloat16)[:, None], covariates)[0]
        ols_coef = newton_solve(ctrl_gram, ctrl_moment)
        coefs = jnp.zeros((covariates.shape[1],), jnp.float32)
        for step in range(NEWTON):
            index = jnp.dot(covariates.astype(jnp.float32), coefs.astype(jnp.bfloat16).astype(jnp.float32), preferred_element_type=jnp.float32)
            probability = jax.nn.sigmoid(index)
            weight = eligible * probability * (1.0 - probability)
            weighted = (weight[:, None] * covariates).astype(jnp.bfloat16)
            curvature = cross_rows(weighted, covariates)
            gradient = cross_rows(((treated - probability) * eligible).astype(jnp.bfloat16)[:, None], covariates)[0]
            coefs = coefs + newton_solve(curvature, gradient)
        residual = change - jnp.dot(covariates.astype(jnp.float32), ols_coef.astype(jnp.bfloat16).astype(jnp.float32), preferred_element_type=jnp.float32)
        odds_ratio = jnp.exp(jnp.dot(covariates.astype(jnp.float32), coefs.astype(jnp.bfloat16).astype(jnp.float32), preferred_element_type=jnp.float32))
        first = jnp.sum(treated)
        second = jnp.sum(treated * residual)
        third = jnp.sum(control * odds_ratio)
        fourth = jnp.sum(control * odds_ratio * residual)
        influence = total_rows * (treated * (residual - second / first) / first - control * odds_ratio * (residual - fourth / third) / third)
        scaled = (influence / math.sqrt(total_rows)).astype(jnp.bfloat16)
        results.append(influence)
        draws_out.append(jnp.dot(scaled[None, :].astype(jnp.float32), multipliers.astype(jnp.float32), preferred_element_type=jnp.float32)[0])
    return (jnp.stack(results), jnp.stack(draws_out))
```

```python
import math

import jax
import jax.numpy as jnp
from jax import lax
from jax.sharding import Mesh, PartitionSpec as P

NEWTON = 3
ROWS = ("y", "z", "core")
F32 = jnp.float32
BF16 = jnp.bfloat16


def cross_rows(left, right):
    return lax.dot_general(left, right, (((0,), (0,)), ((), ())), preferred_element_type=F32)


def solve(matrix, vector):
    factor = jnp.linalg.cholesky(matrix)
    return jax.scipy.linalg.cho_solve((factor, True), vector.reshape(-1, 1)).reshape(-1)


def swap_cores(value):
    return lax.ppermute(value, "core", [(0, 1), (1, 0)])


def all_sum(value):
    half = value.shape[0] // 2
    core = lax.axis_index("core")
    peers = lax.axis_size(("y", "z"))
    mine = lax.dynamic_slice_in_dim(value, core * half, half)
    theirs = lax.dynamic_slice_in_dim(value, (1 - core) * half, half)
    mine = mine + swap_cores(theirs)
    copies = lax.optimization_barrier(jnp.broadcast_to(mine[None], (peers,) + mine.shape))
    arrived = lax.all_to_all(copies, ("y", "z"), 0, 0)
    total = jnp.sum(arrived, axis=0)
    other = swap_cores(total)
    first = jnp.where(core == 0, total, other)
    second = jnp.where(core == 0, other, total)
    return jnp.concatenate([first, second], axis=0)


def rows_of(parts, rows):
    value = jnp.concatenate([p.reshape(-1, 128) for p in parts], axis=0)
    return jnp.pad(value, ((0, rows - value.shape[0]), (0, 0)))


def lanes(*scalars):
    return jnp.pad(jnp.stack(scalars), (0, 128 - len(scalars)))


def shards(covariates, outcomes, multipliers, cohorts, cells):
    rows_here = covariates.shape[0]
    total_rows = rows_here * lax.axis_size(ROWS)
    block_rows = rows_here // cohorts.shape[0]
    cohort_rows = jnp.broadcast_to(cohorts[:, None], (cohorts.shape[0], block_rows)).reshape(-1)
    treat_group = cells[0, 0]
    period = cells[0, 1]
    treated = (cohort_rows == treat_group).astype(F32)
    control = (cohort_rows > period).astype(F32)
    eligible = treated + control
    change = outcomes[period] - outcomes[treat_group - 1]
    ctrl_x = control.astype(BF16)[:, None] * covariates
    ctrl_gram = cross_rows(ctrl_x, covariates)
    ctrl_moment = cross_rows((control * change).astype(BF16)[:, None], covariates)[0]
    elig_x = eligible.astype(BF16)[:, None] * covariates
    elig_gram = cross_rows(elig_x, covariates)
    treat_x = cross_rows(treated.astype(BF16)[:, None], covariates)[0]
    treat_change = jnp.sum(treated * change)
    summed = all_sum(
        rows_of([ctrl_gram, elig_gram, ctrl_moment, treat_x, lanes(treat_change)], 272)
    )
    ctrl_gram, elig_gram = summed[:128], summed[128:256]
    ctrl_moment, treat_x, treat_change = summed[256], summed[257], summed[258, 0]
    count = treat_x[0]
    ols_coef = solve(ctrl_gram, ctrl_moment).astype(BF16)
    coefs = solve(0.25 * elig_gram, 0.5 * (treat_x - ctrl_gram[0]))
    mean_treated = (treat_change - jnp.sum(treat_x * ols_coef.astype(F32))) / count
    for step in range(NEWTON - 1):
        index = jnp.dot(covariates, coefs.astype(BF16), preferred_element_type=F32)
        probability = jax.nn.sigmoid(index)
        weight = eligible * probability * (1.0 - probability)
        weighted = (weight[:, None] * covariates).astype(BF16)
        curvature = cross_rows(weighted, covariates)
        gradient = cross_rows(((treated - probability) * eligible).astype(BF16)[:, None], covariates)[0]
        summed = all_sum(rows_of([curvature, gradient], 144))
        coefs = coefs + solve(summed[:128], summed[128])
    residual = change - jnp.dot(covariates, ols_coef, preferred_element_type=F32)
    odds_ratio = jnp.exp(jnp.dot(covariates, coefs.astype(BF16), preferred_element_type=F32))
    own_treated = treated * (residual - mean_treated) / count
    own_odds = control * odds_ratio
    own_product = own_odds * residual
    split = []
    for row in (own_treated, own_product, own_odds):
        high = lax.reduce_precision(row, 8, 7)
        split += [high.astype(BF16), (row - high).astype(BF16)]
    every_cell = lax.all_gather(jnp.stack(split), "cell", axis=0)
    cell_count = every_cell.shape[0]
    draws = jnp.dot(every_cell.reshape(-1, rows_here), multipliers, preferred_element_type=F32)
    draws = draws.reshape(cell_count, 3, 2, -1).sum(axis=2)
    sums = lax.all_gather(jnp.stack([jnp.sum(own_odds), jnp.sum(own_product)]), "cell", axis=0)
    summed = all_sum(rows_of([draws, lanes(*sums.reshape(-1))], 16))
    draws = summed[:12].reshape(cell_count, 3, 128)
    sums = summed[12, : 2 * cell_count].reshape(cell_count, 2)
    weight_sum = sums[:, 0:1]
    mean_control = sums[:, 1:2] / weight_sum
    bootstrap = math.sqrt(total_rows) * (
        draws[:, 0] - (draws[:, 1] - mean_control * draws[:, 2]) / weight_sum
    )
    cell = lax.axis_index("cell")
    influence = total_rows * (
        own_treated - (own_product - mean_control[cell, 0] * own_odds) / weight_sum[cell, 0]
    )
    return (influence[None, :], bootstrap)


def solution(mesh):
    shape = dict(mesh.shape)
    fine = Mesh(mesh.devices.reshape(4, 8, 2, shape["cell"]), ROWS + ("cell",))
    return jax.shard_map(
        shards,
        mesh=fine,
        in_specs=(P(ROWS, None), P(None, ROWS), P(ROWS, "cell"), P(ROWS), P("cell", None)),
        out_specs=(P("cell", ROWS), P(None, "cell")),
        check_vma=False,
    )
```

```python
import functools
import math

import jax
import jax.numpy as jnp
from jax import lax
from jax.experimental import pallas as pl
from jax.experimental.pallas import tpu as pltpu
from jax.sharding import Mesh, PartitionSpec as P

ROWS = ("y", "z", "core")
F32 = jnp.float32
BF16 = jnp.bfloat16
WIDTH = 128
HALF = 64
CHUNK = 2048
PACKED = 40
VMEM = pl.BlockSpec(memory_space=pltpu.VMEM)
SMEM = pl.BlockSpec(memory_space=pltpu.SMEM)
ANY = pl.BlockSpec(memory_space=pl.ANY)
PARAMS = pltpu.CompilerParams(vmem_limit_bytes=24 << 20)


def shape(*dims, dtype=F32):
    return jax.ShapeDtypeStruct(dims, dtype)


def iota(dims, axis):
    return lax.broadcasted_iota(jnp.int32, dims, axis)


def fold(gram):
    top, low = gram[:HALF], gram[HALF:]
    row, col = iota((HALF, WIDTH), 0), iota((HALF, WIDTH), 1)
    folded = jnp.where((col < HALF) & (col > row), pltpu.roll(low, HALF, 1), top)
    diagonal = jnp.sum(jnp.where(col - HALF == row, low, 0.0), axis=0, keepdims=True)
    return folded, diagonal


def unfold(folded, diagonal):
    row, col = iota((HALF, WIDTH), 0), iota((HALF, WIDTH), 1)
    turned = jnp.concatenate([folded, jnp.zeros_like(folded)], axis=0).T
    top = jnp.where((col >= HALF) | (col <= row), folded, turned[:HALF])
    right = col - HALF
    low = jnp.where(
        right > row,
        pltpu.roll(folded, HALF, 1),
        jnp.where(right < row, pltpu.roll(turned[:HALF], HALF, 1), diagonal),
    )
    return top, jnp.where(col < HALF, turned[HALF:], low)


def write_payload(out, folded, extras):
    pad = jnp.zeros((7, WIDTH), F32)
    for p in range(out.shape[0]):
        h = p % 2
        out[p, 0:32, :] = folded[32 * h : 32 * h + 32]
        out[p, 32:40, :] = jnp.concatenate([extras[h], pad], axis=0)


def summed(ref):
    total = ref[0]
    for p in range(1, ref.shape[0]):
        total = total + ref[p]
    return total


def lane(block, i):
    return jnp.broadcast_to(block[:, i : i + 1], block.shape)


def sub(block, i):
    return jnp.broadcast_to(block[i : i + 1, :], block.shape)


def scaled_panel(panel, k):
    row, col = iota((8, WIDTH), 0), iota((8, WIDTH), 1) - 8 * k
    inside = (col >= 0) & (col < 8)
    columns = [lane(panel, 8 * k + j) for j in range(8)]
    out = jnp.where(inside, jnp.where(col == row, 1.0, 0.0), panel)
    for j in range(8):
        inverse = 1.0 / sub(columns[j], j)
        here = row == j
        factor = jnp.where(here, 0.0, columns[j])

        def step(block):
            pivot = sub(block, j) * inverse
            return jnp.where(here, pivot, block) - factor * pivot

        out = step(out)
        for m in range(j + 1, 8):
            columns[m] = step(columns[m])
    return out, inside


def swept(blocks):
    count = len(blocks)
    for k in range(count):
        scaled, inside = scaled_panel(blocks[k], k)
        new = []
        for i in range(count):
            if i == k:
                new.append(jnp.where(inside, -scaled, scaled))
                continue
            change = lane(blocks[i], 8 * k) * sub(scaled, 0)
            for j in range(1, 8):
                change = change + lane(blocks[i], 8 * k + j) * sub(scaled, j)
            new.append(jnp.where(inside, change, blocks[i] - change))
        blocks = new
    return blocks


def solve(top, low, vector):
    blocks = [top[8 * i : 8 * i + 8] for i in range(8)] + [low[8 * i : 8 * i + 8] for i in range(8)]
    inverse = jnp.concatenate(swept(blocks), axis=0)
    return -jnp.dot(
        jnp.broadcast_to(vector, (8, WIDTH)),
        inverse,
        precision=lax.Precision.HIGHEST,
        preferred_element_type=F32,
    )


def halves(core, own, other):
    is_first = core == 0
    first = jnp.where(is_first, own, other)
    second = jnp.where(is_first, other, own)
    folded = jnp.concatenate([first[:32], second[:32]], axis=0)
    return folded, first[32:33], second[32:33]


def arrivals(source, target, sems, axis):
    copies = []
    for i in range(target.shape[axis] // CHUNK):
        span = pl.ds(i * CHUNK, CHUNK)
        place = (span, slice(None)) if axis == 0 else (slice(None), span)
        copies.append(pltpu.make_async_copy(source.at[place], target.at[place], sems.at[i]))
        copies[-1].start()
    return copies


def chunk_of(i):
    return slice(i * CHUNK, (i + 1) * CHUNK)


def flag(condition, dtype=F32):
    return jnp.where(condition, 1.0, 0.0).astype(dtype)


def first_kernel(cells, cohorts, x_hbm, y_hbm, xt_hbm, out, x, y, xt, x_sems, y_sems, xt_sems):
    group, period = cells[0, 0], cells[0, 1]
    per = CHUNK // WIDTH
    x_copies = arrivals(x_hbm, x, x_sems, 0)
    y_copies = arrivals(y_hbm, y, y_sems, 1)
    total = jnp.zeros((WIDTH + 16, WIDTH), F32)
    changes = jnp.zeros((1, WIDTH), F32)
    sent = []
    for i, copy in enumerate(x_copies):
        span = pl.ds(i * CHUNK, CHUNK)
        copy.wait()
        here = x[chunk_of(i), :]
        turned = here.T
        xt[:, chunk_of(i)] = turned
        sent.append(pltpu.make_async_copy(xt.at[:, span], xt_hbm.at[:, span], xt_sems.at[i]))
        sent[-1].start()
        left, marks = [], []
        for b in range(per):
            cohort = cohorts[i * per + b]
            treated = flag(cohort == group)
            eligible = treated + flag(cohort > period)
            left.append(turned[:, b * WIDTH : (b + 1) * WIDTH] * eligible.astype(BF16))
            marks.append(jnp.full((16, WIDTH), treated, F32).astype(BF16))
        left = jnp.concatenate([jnp.concatenate(left, axis=1), jnp.concatenate(marks, axis=1)], axis=0)
        total = total + jnp.dot(left, here, preferred_element_type=F32)
    for copy in y_copies:
        copy.wait()
    change = y[pl.ds(period, 1), :] - y[pl.ds(group - 1, 1), :]
    for b in range(cohorts.shape[0]):
        changes = changes + flag(cohorts[b] == group) * change[:, b * WIDTH : (b + 1) * WIDTH]
    folded, diagonal = fold(total[:WIDTH])
    scalar = jnp.sum(changes, axis=1, keepdims=True)
    first_lane = iota((1, WIDTH), 1) == 0
    write_payload(out, folded, (total[WIDTH : WIDTH + 1], jnp.where(first_lane, scalar, diagonal)))
    for copy in sent:
        copy.wait()


def control_kernel(cells, cohorts, x_hbm, xt_hbm, y, out, x, xt, x_sems, xt_sems):
    group, period = cells[0, 0], cells[0, 1]
    per = CHUNK // WIDTH
    x_copies = arrivals(x_hbm, x, x_sems, 0)
    xt_copies = arrivals(xt_hbm, xt, xt_sems, 1)
    total = jnp.zeros((WIDTH + 16, WIDTH), F32)
    for i in range(len(x_copies)):
        span = pl.ds(i * CHUNK, CHUNK)
        change = y[pl.ds(period, 1), span] - y[pl.ds(group - 1, 1), span]
        change = jnp.broadcast_to(change, (16, CHUNK)).astype(BF16)
        x_copies[i].wait()
        xt_copies[i].wait()
        turned = jnp.concatenate([xt[:, chunk_of(i)], change], axis=0)
        left = []
        for b in range(per):
            control = flag(cohorts[i * per + b] > period).astype(BF16)
            left.append(turned[:, b * WIDTH : (b + 1) * WIDTH] * control)
        left = jnp.concatenate(left, axis=1)
        total = total + jnp.dot(left, x[chunk_of(i), :], preferred_element_type=F32)
    folded, diagonal = fold(total[:WIDTH])
    out[0:64, :] = folded
    out[64:72, :] = jnp.concatenate(
        [total[WIDTH : WIDTH + 1], diagonal, jnp.zeros((6, WIDTH), F32)], axis=0
    )


def newton_kernel(
    first, cells, cohorts, own, other, x_hbm, xt_hbm, before, control, coefs, keep, out, x, xt, x_sems, xt_sems
):
    group, period = cells[0, 0], cells[0, 1]
    per = CHUNK // WIDTH
    xt_copies = arrivals(xt_hbm, xt, xt_sems, 1)
    x_copies = arrivals(x_hbm, x, x_sems, 0)
    mine = summed(own)
    folded, row, diagonal = halves(lax.axis_index("core"), mine[:40], summed(other)[:40])
    top, low = unfold(folded, diagonal)
    if first:
        keep[...] = jnp.concatenate([row, diagonal, jnp.zeros((6, WIDTH), F32)], axis=0)
        new = 4.0 * solve(top, low, row - 0.5 * top[0:1])
    else:
        keep[...] = mine[32:40]
        new = before[...] + solve(top, low, row)
    coefs[...] = new
    rounded = jnp.concatenate([new, new], axis=0).astype(BF16)
    total = jnp.zeros((WIDTH + 16, WIDTH), F32)
    for i in range(len(x_copies)):
        xt_copies[i].wait()
        turned = xt[:, chunk_of(i)]
        index = jnp.dot(rounded, turned, preferred_element_type=F32)
        probability = jax.nn.sigmoid(index)
        weight = probability * (1.0 - probability)
        left, errors = [], []
        for b in range(per):
            cohort = cohorts[i * per + b]
            treated = flag(cohort == group)
            eligible = treated + flag(cohort > period)
            span = slice(b * WIDTH, (b + 1) * WIDTH)
            here = jnp.broadcast_to(weight[0:1, span] * eligible, (WIDTH, WIDTH))
            left.append((here * turned[:, span].astype(F32)).astype(BF16))
            errors.append(((treated - probability[:, span]) * eligible).astype(BF16))
        left = jnp.concatenate([jnp.concatenate(left, axis=1), jnp.concatenate(errors, axis=1)], axis=0)
        x_copies[i].wait()
        total = total + jnp.dot(left, x[chunk_of(i), :], preferred_element_type=F32)
    folded, diagonal = fold(total[:WIDTH])
    write_payload(out, folded, (total[WIDTH : WIDTH + 1], diagonal))
    for p in range(out.shape[0]):
        if first:
            out[p, 33:35, :] = control[64:66, :]
            out[p, 40:48, :] = control[8 * p : 8 * p + 8, :]
        else:
            out[p, 40:48, :] = mine[40:48]


def control_solve_kernel(arrived, extras, out):
    folded = jnp.concatenate([arrived[p, 40:48, :] for p in range(arrived.shape[0])], axis=0)
    solved = solve(*unfold(folded, extras[2:3, :]), extras[1:2, :])
    out[...] = solved.astype(BF16).astype(F32)


def last_kernel(cells, own, other, control, before, keep, out):
    folded, row, diagonal = halves(lax.axis_index("core"), summed(own), summed(other))
    new = before[...] + solve(*unfold(folded, diagonal), row)
    ols = control[0:1, :]
    treated_x = keep[0:1, :]
    count = lane(treated_x, 0)
    fitted = jnp.sum(ols * treated_x, axis=1, keepdims=True)
    mean = (lane(keep[1:2, :], 0) - fitted) / count
    out[...] = jnp.concatenate(
        [
            new[0:1].astype(BF16).astype(F32),
            ols,
            mean,
            count,
            jnp.full((1, WIDTH), cells[0, 0].astype(F32), F32),
            jnp.full((1, WIDTH), cells[0, 1].astype(F32), F32),
            jnp.zeros((2, WIDTH), F32),
        ],
        axis=0,
    )


def draws_kernel(
    cohorts, m0, m1, m2, m3, xt_hbm, y_hbm, mult_hbm, out, treated_out, product_out, odds_out,
    xt, y, mult, xt_sems, y_sems, mult_sems,
):
    per = CHUNK // WIDTH
    xt_copies = arrivals(xt_hbm, xt, xt_sems, 1)
    y_copies = arrivals(y_hbm, y, y_sems, 1)
    mult_copies = arrivals(mult_hbm, mult, mult_sems, 0)
    blank = jnp.zeros((4, WIDTH), F32)

    def stacked(i):
        return jnp.concatenate([m[i : i + 1, :] for m in (m0, m1, m2, m3)] + [blank], axis=0)

    left = jnp.concatenate([stacked(0), stacked(1)], axis=0).astype(BF16)
    mean, count, group, period = stacked(2), stacked(3), stacked(4), stacked(5)
    valid = iota((8, WIDTH), 0) < 4
    per_count = jnp.where(valid, 1.0 / jnp.where(valid, count, 1.0), 0.0)
    group = jnp.where(valid, group, -1.0)
    period = jnp.where(valid, period, 99.0)
    signs = [flag(period == p) - flag(group - 1.0 == p) for p in range(8)]
    total = jnp.zeros((48, WIDTH), F32)
    odds_sum = jnp.zeros((8, WIDTH), F32)
    product_sum = jnp.zeros((8, WIDTH), F32)
    for i in range(len(xt_copies)):
        xt_copies[i].wait()
        both = jnp.dot(left, xt[:, chunk_of(i)], preferred_element_type=F32)
        y_copies[i].wait()
        parts = []
        for b in range(per):
            span = slice(b * WIDTH, (b + 1) * WIDTH)
            place = slice(i * CHUNK + b * WIDTH, i * CHUNK + (b + 1) * WIDTH)
            cohort = cohorts[i * per + b].astype(F32)
            outcome = y[:, place]
            change = signs[0] * sub(outcome, 0)
            for p in range(1, 8):
                change = change + signs[p] * sub(outcome, p)
            residual = change - both[8:16, span]
            treated = jnp.where(group == cohort, (residual - mean) * per_count, 0.0)
            odds = jnp.where(period < cohort, jnp.exp(both[0:8, span]), 0.0)
            product = odds * residual
            odds_sum = odds_sum + odds
            product_sum = product_sum + product
            treated_out[:, place] = treated[0:1]
            product_out[:, place] = product[0:1]
            odds_out[:, place] = odds[0:1]
            pairs = []
            for value in (treated, product, odds):
                high = value.astype(BF16).astype(F32)
                pairs.append(jnp.concatenate([high, value - high], axis=0).astype(BF16))
            parts.append(jnp.concatenate(pairs, axis=0))
        mult_copies[i].wait()
        total = total + jnp.dot(
            jnp.concatenate(parts, axis=1), mult[chunk_of(i), :], preferred_element_type=F32
        )
    col = iota((8, WIDTH), 1)
    both = jnp.where(
        col == 0,
        jnp.sum(odds_sum, axis=1, keepdims=True),
        jnp.where(col == 1, jnp.sum(product_sum, axis=1, keepdims=True), 0.0),
    )
    rows = [(total[16 * s : 16 * s + 8] + total[16 * s + 8 : 16 * s + 16])[0:4] for s in range(3)]
    rows = jnp.concatenate(rows + [both[0:4]], axis=0)
    for p in range(out.shape[0]):
        out[p] = rows


def relay_kernel(arrived, out):
    rows = out.shape[1]
    total = summed(arrived)[:rows]
    for p in range(out.shape[0]):
        out[p] = total


def finish_kernel(total_rows, arrived, treated, product, odds, influence, bootstrap):
    cell = lax.axis_index("cell")
    sums = summed(arrived)
    weight = lane(sums[12:16], 0)
    mean = lane(sums[12:16], 1) / weight
    draws = math.sqrt(total_rows) * (sums[0:4] - (sums[4:8] - mean * sums[8:12]) / weight)
    for slot in range(4):
        bootstrap[pl.ds(cell ^ slot, 1), :] = draws[slot : slot + 1]
    scale = total_rows / weight[0:1, 0:1]
    influence[...] = total_rows * treated[...] - scale * (product[...] - mean[0:1, 0:1] * odds[...])


def swap_cores(value):
    return lax.ppermute(value, "core", [(0, 1), (1, 0)])


def to_pairs(payload):
    return lax.all_to_all(payload, ("y", "core"), 0, 0)


def to_line(arrived, rows):
    peers = lax.axis_size("z")
    copies = call(relay_kernel, "relay", [shape(peers, rows, WIDTH)], [VMEM])(arrived)
    return lax.all_to_all(copies[0], "z", 0, 0)


def call(kernel, name, outs, ins, out_specs=None, scratch=(), cost=None):
    return pl.pallas_call(
        kernel,
        out_shape=outs,
        in_specs=ins,
        out_specs=out_specs or [VMEM] * len(outs),
        scratch_shapes=list(scratch),
        compiler_params=PARAMS,
        cost_estimate=cost,
        name=name,
    )


def shards(covariates, outcomes, multipliers, cohorts, cells):
    rows_here = covariates.shape[0]
    total_rows = rows_here * lax.axis_size(ROWS)
    pairs = lax.axis_size(("y", "core"))
    sems = pltpu.SemaphoreType.DMA((rows_here // CHUNK,))
    tall = pltpu.VMEM((rows_here, WIDTH), BF16)
    wide = pltpu.VMEM((WIDTH, rows_here), BF16)
    deep = pltpu.VMEM(outcomes.shape, F32)
    vector = shape(1, rows_here)
    eight = shape(8, WIDTH)
    turned, payload = call(
        first_kernel,
        "first",
        [shape(WIDTH, rows_here, dtype=BF16), shape(pairs, 40, WIDTH)],
        [SMEM, SMEM, ANY, ANY],
        [ANY, VMEM],
        [tall, deep, wide, sems, sems, sems],
    )(cells, cohorts, covariates, outcomes)
    arrived = to_line(to_pairs(payload), 40)
    control = call(
        control_kernel,
        "control",
        [shape(72, WIDTH)],
        [SMEM, SMEM, ANY, ANY, VMEM],
        None,
        [tall, wide, sems, sems],
        pl.CostEstimate(flops=1 << 33, bytes_accessed=10 << 20, transcendentals=0),
    )(cells, cohorts, covariates, turned, outcomes)[0]
    coefs = jnp.zeros((8, WIDTH), F32)
    kept = []
    for step in range(2):
        coefs, keep, payload = call(
            functools.partial(newton_kernel, step == 0),
            "newton",
            [eight, eight, shape(pairs, 48, WIDTH)],
            [SMEM, SMEM, VMEM, VMEM, ANY, ANY, VMEM, VMEM],
            None,
            [tall, wide, sems, sems],
        )(cells, cohorts, arrived, swap_cores(arrived), covariates, turned, coefs, control)
        kept.append(keep)
        halfway = to_pairs(payload)
        arrived = to_line(halfway, 48 if step == 0 else 40)
    ols = call(
        control_solve_kernel,
        "ols",
        [eight],
        [VMEM, VMEM],
        cost=pl.CostEstimate(flops=1 << 33, bytes_accessed=10 << 20, transcendentals=0),
    )(halfway, kept[1])[0]
    message = call(last_kernel, "last", [eight], [SMEM] + [VMEM] * 5)(
        cells, arrived, swap_cores(arrived), ols, coefs, kept[0]
    )[0]
    messages = [message] + [
        lax.ppermute(message, "cell", [(i, i ^ s) for i in range(4)]) for s in range(1, 4)
    ]
    payload, treated, product, odds = call(
        draws_kernel,
        "draws",
        [shape(pairs, 16, WIDTH), vector, vector, vector],
        [SMEM] + [VMEM] * 4 + [ANY] * 3,
        None,
        [wide, deep, tall, sems, sems, sems],
    )(cohorts, *messages, turned, outcomes, multipliers)
    arrived = to_line(to_pairs(payload), 16)
    return call(
        functools.partial(finish_kernel, total_rows),
        "finish",
        [vector, shape(4, WIDTH)],
        [VMEM] * 4,
    )(arrived, treated, product, odds)


def solution(mesh):
    fine = Mesh(mesh.devices.reshape(4, 8, 2, 4), ROWS + ("cell",))
    return jax.shard_map(
        shards,
        mesh=fine,
        in_specs=(P(ROWS, None), P(None, ROWS), P(ROWS, "cell"), P(ROWS), P("cell", None)),
        out_specs=(P("cell", ROWS), P(None, "cell")),
        check_vma=False,
    )
```

```python
import functools
import math

import jax
import jax.numpy as jnp
from jax import lax
from jax.experimental import pallas as pl
from jax.experimental.pallas import tpu as pltpu
from jax.sharding import Mesh, PartitionSpec as P

ROWS = ("y", "z", "core")
F32 = jnp.float32
BF16 = jnp.bfloat16
WIDTH = 128
HALF = 64
CHUNK = 2048
PACKED = 40
VMEM = pl.BlockSpec(memory_space=pltpu.VMEM)
SMEM = pl.BlockSpec(memory_space=pltpu.SMEM)
HBM = pl.BlockSpec(memory_space=pltpu.HBM)
FREE = pl.BlockSpec()
PARAMS = pltpu.CompilerParams(vmem_limit_bytes=24 << 20)


def shape(*dims, dtype=F32):
    return jax.ShapeDtypeStruct(dims, dtype)


def iota(dims, axis):
    return lax.broadcasted_iota(jnp.int32, dims, axis)


def fold(gram):
    top, low = gram[:HALF], gram[HALF:]
    row, col = iota((HALF, WIDTH), 0), iota((HALF, WIDTH), 1)
    folded = jnp.where((col < HALF) & (col > row), pltpu.roll(low, HALF, 1), top)
    diagonal = jnp.sum(jnp.where(col - HALF == row, low, 0.0), axis=0, keepdims=True)
    return folded, diagonal


def unfold(folded, diagonal):
    row, col = iota((HALF, WIDTH), 0), iota((HALF, WIDTH), 1)
    turned = jnp.concatenate([folded, jnp.zeros_like(folded)], axis=0).T
    top = jnp.where((col >= HALF) | (col <= row), folded, turned[:HALF])
    right = col - HALF
    low = jnp.where(
        right > row,
        pltpu.roll(folded, HALF, 1),
        jnp.where(right < row, pltpu.roll(turned[:HALF], HALF, 1), diagonal),
    )
    return top, jnp.where(col < HALF, turned[HALF:], low)


def write_payload(out, folded, extras):
    pad = jnp.zeros((7, WIDTH), F32)
    for p in range(out.shape[0]):
        h = p % 2
        out[p, 0:32, :] = folded[32 * h : 32 * h + 32]
        out[p, 32:40, :] = jnp.concatenate([extras[h], pad], axis=0)


def summed(ref):
    total = ref[0]
    for p in range(1, ref.shape[0]):
        total = total + ref[p]
    return total


def lane(block, i):
    return jnp.broadcast_to(block[:, i : i + 1], block.shape)


def sub(block, i):
    return jnp.broadcast_to(block[i : i + 1, :], block.shape)


def scaled_panel(panel, k):
    row, col = iota((8, WIDTH), 0), iota((8, WIDTH), 1) - 8 * k
    inside = (col >= 0) & (col < 8)
    columns = [lane(panel, 8 * k + j) for j in range(8)]
    out = jnp.where(inside, jnp.where(col == row, 1.0, 0.0), panel)
    for j in range(8):
        inverse = 1.0 / sub(columns[j], j)
        here = row == j
        factor = jnp.where(here, 0.0, columns[j])

        def step(block):
            pivot = sub(block, j) * inverse
            return jnp.where(here, pivot, block) - factor * pivot

        out = step(out)
        for m in range(j + 1, 8):
            columns[m] = step(columns[m])
    return out, inside


def swept(blocks):
    count = len(blocks)
    for k in range(count):
        scaled, inside = scaled_panel(blocks[k], k)
        new = []
        for i in range(count):
            if i == k:
                new.append(jnp.where(inside, -scaled, scaled))
                continue
            change = lane(blocks[i], 8 * k) * sub(scaled, 0)
            for j in range(1, 8):
                change = change + lane(blocks[i], 8 * k + j) * sub(scaled, j)
            new.append(jnp.where(inside, change, blocks[i] - change))
        blocks = new
    return blocks


def solve(top, low, vector):
    blocks = [top[8 * i : 8 * i + 8] for i in range(8)] + [low[8 * i : 8 * i + 8] for i in range(8)]
    inverse = jnp.concatenate(swept(blocks), axis=0)
    return -jnp.dot(
        jnp.broadcast_to(vector, (8, WIDTH)),
        inverse,
        precision=lax.Precision.HIGHEST,
        preferred_element_type=F32,
    )


def halves(core, own, other):
    is_first = core == 0
    first = jnp.where(is_first, own, other)
    second = jnp.where(is_first, other, own)
    folded = jnp.concatenate([first[:32], second[:32]], axis=0)
    return folded, first[32:33], second[32:33]


def arrivals(source, target, sems, axis):
    copies = []
    for i in range(target.shape[axis] // CHUNK):
        span = pl.ds(i * CHUNK, CHUNK)
        place = (span, slice(None)) if axis == 0 else (slice(None), span)
        copies.append(pltpu.make_async_copy(source.at[place], target.at[place], sems.at[i]))
        copies[-1].start()
    return copies


def chunk_of(i):
    return slice(i * CHUNK, (i + 1) * CHUNK)


def flag(condition, dtype=F32):
    return jnp.where(condition, 1.0, 0.0).astype(dtype)


def first_kernel(
    cells_hbm, cohorts_hbm, x_hbm, y_hbm, x, xt, xt_hbm, out, cells, cohorts, y, x_sems, y_sems, xt_sems, sems
):
    per = CHUNK // WIDTH
    small = [
        pltpu.make_async_copy(cells_hbm, cells, sems.at[0]),
        pltpu.make_async_copy(cohorts_hbm, cohorts, sems.at[1]),
    ]
    for copy in small:
        copy.start()
    x_copies = arrivals(x_hbm, x, x_sems, 0)
    y_copies = arrivals(y_hbm, y, y_sems, 1)
    for copy in small:
        copy.wait()
    group, period = cells[0, 0], cells[0, 1]
    total = jnp.zeros((WIDTH + 16, WIDTH), F32)
    changes = jnp.zeros((1, WIDTH), F32)
    sent = []
    for i, copy in enumerate(x_copies):
        copy.wait()
        here = x[chunk_of(i), :]
        turned = here.T
        xt[:, chunk_of(i)] = turned
        span = pl.ds(i * CHUNK, CHUNK)
        sent.append(pltpu.make_async_copy(xt.at[:, span], xt_hbm.at[:, span], xt_sems.at[i]))
        sent[-1].start()
        left, marks = [], []
        for b in range(per):
            cohort = cohorts[i * per + b]
            treated = flag(cohort == group)
            eligible = treated + flag(cohort > period)
            left.append(turned[:, b * WIDTH : (b + 1) * WIDTH] * eligible.astype(BF16))
            marks.append(jnp.full((16, WIDTH), treated, F32).astype(BF16))
        left = jnp.concatenate([jnp.concatenate(left, axis=1), jnp.concatenate(marks, axis=1)], axis=0)
        total = total + jnp.dot(left, here, preferred_element_type=F32)
    for copy in y_copies:
        copy.wait()
    change = y[pl.ds(period, 1), :] - y[pl.ds(group - 1, 1), :]
    for b in range(cohorts.shape[0]):
        changes = changes + flag(cohorts[b] == group) * change[:, b * WIDTH : (b + 1) * WIDTH]
    folded, diagonal = fold(total[:WIDTH])
    scalar = jnp.sum(changes, axis=1, keepdims=True)
    first_lane = iota((1, WIDTH), 1) == 0
    write_payload(out, folded, (total[WIDTH : WIDTH + 1], jnp.where(first_lane, scalar, diagonal)))
    for copy in sent:
        copy.wait()


def control_kernel(cells, cohorts, x, xt, y, out):
    group, period = cells[0, 0], cells[0, 1]
    per = CHUNK // WIDTH
    total = jnp.zeros((WIDTH + 16, WIDTH), F32)
    for i in range(x.shape[0] // CHUNK):
        span = pl.ds(i * CHUNK, CHUNK)
        change = y[pl.ds(period, 1), span] - y[pl.ds(group - 1, 1), span]
        change = jnp.broadcast_to(change, (16, CHUNK)).astype(BF16)
        turned = jnp.concatenate([xt[:, chunk_of(i)], change], axis=0)
        left = []
        for b in range(per):
            control = flag(cohorts[i * per + b] > period).astype(BF16)
            left.append(turned[:, b * WIDTH : (b + 1) * WIDTH] * control)
        left = jnp.concatenate(left, axis=1)
        total = total + jnp.dot(left, x[chunk_of(i), :], preferred_element_type=F32)
    folded, diagonal = fold(total[:WIDTH])
    out[0:64, :] = folded
    out[64:72, :] = jnp.concatenate(
        [total[WIDTH : WIDTH + 1], diagonal, jnp.zeros((6, WIDTH), F32)], axis=0
    )


def newton_kernel(
    first, cells, cohorts, own, other, x, xt, before, control, coefs, keep, out
):
    group, period = cells[0, 0], cells[0, 1]
    per = CHUNK // WIDTH
    mine = summed(own)
    folded, row, diagonal = halves(lax.axis_index("core"), mine[:40], summed(other)[:40])
    top, low = unfold(folded, diagonal)
    if first:
        keep[...] = jnp.concatenate([row, diagonal, jnp.zeros((6, WIDTH), F32)], axis=0)
        new = 4.0 * solve(top, low, row - 0.5 * top[0:1])
    else:
        keep[...] = mine[32:40]
        new = before[...] + solve(top, low, row)
    coefs[...] = new
    rounded = jnp.concatenate([new, new], axis=0).astype(BF16)
    total = jnp.zeros((WIDTH + 16, WIDTH), F32)
    for i in range(x.shape[0] // CHUNK):
        turned = xt[:, chunk_of(i)]
        index = jnp.dot(rounded, turned, preferred_element_type=F32)
        probability = jax.nn.sigmoid(index)
        weight = probability * (1.0 - probability)
        left, errors = [], []
        for b in range(per):
            cohort = cohorts[i * per + b]
            treated = flag(cohort == group)
            eligible = treated + flag(cohort > period)
            span = slice(b * WIDTH, (b + 1) * WIDTH)
            here = jnp.broadcast_to(weight[0:1, span] * eligible, (WIDTH, WIDTH))
            left.append((here * turned[:, span].astype(F32)).astype(BF16))
            errors.append(((treated - probability[:, span]) * eligible).astype(BF16))
        left = jnp.concatenate([jnp.concatenate(left, axis=1), jnp.concatenate(errors, axis=1)], axis=0)
        total = total + jnp.dot(left, x[chunk_of(i), :], preferred_element_type=F32)
    folded, diagonal = fold(total[:WIDTH])
    write_payload(out, folded, (total[WIDTH : WIDTH + 1], diagonal))
    for p in range(out.shape[0]):
        if first:
            out[p, 33:35, :] = control[64:66, :]
            out[p, 40:48, :] = control[8 * p : 8 * p + 8, :]
        else:
            out[p, 40:48, :] = mine[40:48]


def control_solve_kernel(arrived, extras, y_hbm, mult_hbm, out, y, mult, y_sems, mult_sems):
    copies = arrivals(mult_hbm, mult, mult_sems, 0) + arrivals(y_hbm, y, y_sems, 1)
    folded = jnp.concatenate([arrived[p, 40:48, :] for p in range(arrived.shape[0])], axis=0)
    solved = solve(*unfold(folded, extras[2:3, :]), extras[1:2, :])
    out[...] = solved.astype(BF16).astype(F32)
    for copy in copies:
        copy.wait()


def last_kernel(cells, own, other, control, before, keep, xt_hbm, out, xt, xt_sems):
    copies = arrivals(xt_hbm, xt, xt_sems, 1)
    folded, row, diagonal = halves(lax.axis_index("core"), summed(own), summed(other))
    new = before[...] + solve(*unfold(folded, diagonal), row)
    ols = control[0:1, :]
    treated_x = keep[0:1, :]
    count = lane(treated_x, 0)
    fitted = jnp.sum(ols * treated_x, axis=1, keepdims=True)
    mean = (lane(keep[1:2, :], 0) - fitted) / count
    out[...] = jnp.concatenate(
        [
            new[0:1].astype(BF16).astype(F32),
            ols,
            mean,
            count,
            jnp.full((1, WIDTH), cells[0, 0].astype(F32), F32),
            jnp.full((1, WIDTH), cells[0, 1].astype(F32), F32),
            jnp.zeros((2, WIDTH), F32),
        ],
        axis=0,
    )
    for copy in copies:
        copy.wait()


def draws_kernel(
    cohorts, m0, m1, m2, m3, xt, y, mult, out, treated_out, product_out, odds_out
):
    per = CHUNK // WIDTH
    blank = jnp.zeros((4, WIDTH), F32)

    def stacked(i):
        return jnp.concatenate([m[i : i + 1, :] for m in (m0, m1, m2, m3)] + [blank], axis=0)

    left = jnp.concatenate([stacked(0), stacked(1)], axis=0).astype(BF16)
    mean, count, group, period = stacked(2), stacked(3), stacked(4), stacked(5)
    valid = iota((8, WIDTH), 0) < 4
    per_count = jnp.where(valid, 1.0 / jnp.where(valid, count, 1.0), 0.0)
    group = jnp.where(valid, group, -1.0)
    period = jnp.where(valid, period, 99.0)
    signs = [flag(period == p) - flag(group - 1.0 == p) for p in range(8)]
    total = jnp.zeros((48, WIDTH), F32)
    odds_sum = jnp.zeros((8, WIDTH), F32)
    product_sum = jnp.zeros((8, WIDTH), F32)
    for i in range(xt.shape[1] // CHUNK):
        both = jnp.dot(left, xt[:, chunk_of(i)], preferred_element_type=F32)
        parts = []
        for b in range(per):
            span = slice(b * WIDTH, (b + 1) * WIDTH)
            place = slice(i * CHUNK + b * WIDTH, i * CHUNK + (b + 1) * WIDTH)
            cohort = cohorts[i * per + b].astype(F32)
            outcome = y[:, place]
            change = signs[0] * sub(outcome, 0)
            for p in range(1, 8):
                change = change + signs[p] * sub(outcome, p)
            residual = change - both[8:16, span]
            treated = jnp.where(group == cohort, (residual - mean) * per_count, 0.0)
            odds = jnp.where(period < cohort, jnp.exp(both[0:8, span]), 0.0)
            product = odds * residual
            odds_sum = odds_sum + odds
            product_sum = product_sum + product
            treated_out[:, place] = treated[0:1]
            product_out[:, place] = product[0:1]
            odds_out[:, place] = odds[0:1]
            pairs = []
            for value in (treated, product, odds):
                high = value.astype(BF16).astype(F32)
                pairs.append(jnp.concatenate([high, value - high], axis=0).astype(BF16))
            parts.append(jnp.concatenate(pairs, axis=0))
        total = total + jnp.dot(
            jnp.concatenate(parts, axis=1), mult[chunk_of(i), :], preferred_element_type=F32
        )
    col = iota((8, WIDTH), 1)
    both = jnp.where(
        col == 0,
        jnp.sum(odds_sum, axis=1, keepdims=True),
        jnp.where(col == 1, jnp.sum(product_sum, axis=1, keepdims=True), 0.0),
    )
    rows = [(total[16 * s : 16 * s + 8] + total[16 * s + 8 : 16 * s + 16])[0:4] for s in range(3)]
    rows = jnp.concatenate(rows + [both[0:4]], axis=0)
    for p in range(out.shape[0]):
        out[p] = rows


def relay_kernel(arrived, out):
    rows = out.shape[1]
    total = summed(arrived)[:rows]
    for p in range(out.shape[0]):
        out[p] = total


def finish_kernel(total_rows, arrived, treated, product, odds, influence, bootstrap):
    cell = lax.axis_index("cell")
    sums = summed(arrived)
    weight = lane(sums[12:16], 0)
    mean = lane(sums[12:16], 1) / weight
    draws = math.sqrt(total_rows) * (sums[0:4] - (sums[4:8] - mean * sums[8:12]) / weight)
    for slot in range(4):
        bootstrap[pl.ds(cell ^ slot, 1), :] = draws[slot : slot + 1]
    scale = total_rows / weight[0:1, 0:1]
    influence[...] = total_rows * treated[...] - scale * (product[...] - mean[0:1, 0:1] * odds[...])


def swap_cores(value):
    return lax.ppermute(value, "core", [(0, 1), (1, 0)])


def to_pairs(payload):
    return lax.all_to_all(payload, ("y", "core"), 0, 0)


def to_line(arrived, rows):
    peers = lax.axis_size("z")
    copies = call(relay_kernel, "relay", [shape(peers, rows, WIDTH)], [VMEM])(arrived)
    return lax.all_to_all(copies[0], "z", 0, 0)


def call(kernel, name, outs, ins, out_specs=None, scratch=(), cost=None):
    return pl.pallas_call(
        kernel,
        out_shape=outs,
        in_specs=ins,
        out_specs=out_specs or [VMEM] * len(outs),
        scratch_shapes=list(scratch),
        compiler_params=PARAMS,
        cost_estimate=cost,
        name=name,
    )


def shards(covariates, outcomes, multipliers, cohorts, cells):
    rows_here = covariates.shape[0]
    total_rows = rows_here * lax.axis_size(ROWS)
    pairs = lax.axis_size(("y", "core"))
    sems = pltpu.SemaphoreType.DMA((rows_here // CHUNK,))
    vector = shape(1, rows_here)
    eight = shape(8, WIDTH)
    cost = pl.CostEstimate(flops=1 << 33, bytes_accessed=10 << 20, transcendentals=0)
    tall, wide, wide_hbm, payload = call(
        first_kernel,
        "first",
        [
            shape(rows_here, WIDTH, dtype=BF16),
            shape(WIDTH, rows_here, dtype=BF16),
            pltpu.HBM((WIDTH, rows_here), BF16),
            shape(pairs, 40, WIDTH),
        ],
        [HBM] * 4,
        [FREE, FREE, HBM, VMEM],
        [
            pltpu.SMEM(cells.shape, jnp.int32),
            pltpu.SMEM(cohorts.shape, jnp.int32),
            pltpu.VMEM(outcomes.shape, F32),
            sems,
            sems,
            sems,
            pltpu.SemaphoreType.DMA((2,)),
        ],
    )(*(pltpu.with_memory_space_constraint(v, pltpu.HBM) for v in (cells, cohorts, covariates, outcomes)))
    halfway = to_pairs(payload)
    arrived = to_line(halfway, 40)
    control = call(
        control_kernel, "control", [shape(72, WIDTH)], [SMEM, SMEM, FREE, FREE, FREE], cost=cost
    )(cells, cohorts, tall, wide, outcomes)[0]
    coefs = jnp.zeros((8, WIDTH), F32)
    kept = []
    for step in range(2):
        coefs, keep, payload = call(
            functools.partial(newton_kernel, step == 0),
            "newton",
            [eight, eight, shape(pairs, 48, WIDTH)],
            [SMEM, SMEM, VMEM, VMEM, FREE, FREE, VMEM, VMEM],
        )(cells, cohorts, arrived, swap_cores(arrived), tall, wide, coefs, control)
        kept.append(keep)
        halfway = to_pairs(payload)
        arrived = to_line(halfway, 48 if step == 0 else 40)
    far = [pltpu.with_memory_space_constraint(v, pltpu.HBM) for v in (outcomes, multipliers, wide_hbm)]
    ols, deep, mult = call(
        control_solve_kernel,
        "ols",
        [eight, shape(*outcomes.shape), shape(rows_here, WIDTH, dtype=BF16)],
        [VMEM, VMEM, HBM, HBM],
        [VMEM, FREE, FREE],
        [sems, sems],
        cost,
    )(halfway, kept[1], *far[:2])
    arrived, ols = lax.optimization_barrier((arrived, ols))
    message, wide = call(
        last_kernel,
        "last",
        [eight, shape(WIDTH, rows_here, dtype=BF16)],
        [SMEM] + [VMEM] * 5 + [HBM],
        [VMEM, FREE],
        [sems],
    )(cells, arrived, swap_cores(arrived), ols, coefs, kept[0], far[2])
    messages = [message] + [
        lax.ppermute(message, "cell", [(i, i ^ s) for i in range(4)]) for s in range(1, 4)
    ]
    payload, treated, product, odds = call(
        draws_kernel,
        "draws",
        [shape(pairs, 16, WIDTH), vector, vector, vector],
        [SMEM] + [VMEM] * 4 + [FREE] * 3,
    )(cohorts, *messages, wide, deep, mult)
    arrived = to_line(to_pairs(payload), 16)
    return call(
        functools.partial(finish_kernel, total_rows),
        "finish",
        [vector, shape(4, WIDTH)],
        [VMEM] * 4,
    )(arrived, treated, product, odds)


def solution(mesh):
    fine = Mesh(mesh.devices.reshape(4, 8, 2, 4), ROWS + ("cell",))
    return jax.shard_map(
        shards,
        mesh=fine,
        in_specs=(P(ROWS, None), P(None, ROWS), P(ROWS, "cell"), P(ROWS), P("cell", None)),
        out_specs=(P("cell", ROWS), P(None, "cell")),
        check_vma=False,
    )
```

```python
import functools
import math

import jax
import jax.numpy as jnp
from jax import lax
from jax.experimental import pallas as pl
from jax.experimental.pallas import tpu as pltpu
from jax.sharding import Mesh, PartitionSpec as P

ROWS = ("y", "z", "core")
F32 = jnp.float32
BF16 = jnp.bfloat16
WIDTH = 128
HALF = 64
CHUNK = 4096
PACKED = 40
VMEM = pl.BlockSpec(memory_space=pltpu.VMEM)
SMEM = pl.BlockSpec(memory_space=pltpu.SMEM)
HBM = pl.BlockSpec(memory_space=pltpu.HBM)
FREE = pl.BlockSpec()
PARAMS = pltpu.CompilerParams(vmem_limit_bytes=24 << 20)


def shape(*dims, dtype=F32):
    return jax.ShapeDtypeStruct(dims, dtype)


def iota(dims, axis):
    return lax.broadcasted_iota(jnp.int32, dims, axis)


def fold(gram):
    top, low = gram[:HALF], gram[HALF:]
    row, col = iota((HALF, WIDTH), 0), iota((HALF, WIDTH), 1)
    folded = jnp.where((col < HALF) & (col > row), pltpu.roll(low, HALF, 1), top)
    diagonal = jnp.sum(jnp.where(col - HALF == row, low, 0.0), axis=0, keepdims=True)
    return folded, diagonal


def unfold(folded, diagonal):
    row, col = iota((HALF, WIDTH), 0), iota((HALF, WIDTH), 1)
    turned = jnp.concatenate([folded, jnp.zeros_like(folded)], axis=0).T
    top = jnp.where((col >= HALF) | (col <= row), folded, turned[:HALF])
    right = col - HALF
    low = jnp.where(
        right > row,
        pltpu.roll(folded, HALF, 1),
        jnp.where(right < row, pltpu.roll(turned[:HALF], HALF, 1), diagonal),
    )
    return top, jnp.where(col < HALF, turned[HALF:], low)


def write_payload(out, folded, extras):
    pad = jnp.zeros((7, WIDTH), F32)
    for p in range(out.shape[0]):
        h = p % 2
        out[p, 0:32, :] = folded[32 * h : 32 * h + 32]
        out[p, 32:40, :] = jnp.concatenate([extras[h], pad], axis=0)


def summed(ref):
    total = ref[0]
    for p in range(1, ref.shape[0]):
        total = total + ref[p]
    return total


def lane(block, i):
    return jnp.broadcast_to(block[:, i : i + 1], block.shape)


def sub(block, i):
    return jnp.broadcast_to(block[i : i + 1, :], block.shape)


def tree(terms):
    while len(terms) > 1:
        terms = [terms[i] + terms[i + 1] for i in range(0, len(terms), 2)]
    return terms[0]


def solve(top, low, vector):
    blocks = [top[8 * i : 8 * i + 8] for i in range(8)] + [low[8 * i : 8 * i + 8] for i in range(8)]
    blocks.append(jnp.broadcast_to(vector, (8, WIDTH)))
    row = iota((8, WIDTH), 0)
    columns = [lane(blocks[0], m) for m in range(8)]
    for k in range(16):
        col = iota((8, WIDTH), 1) - 8 * k
        inside = (col >= 0) & (col < 8)
        scaled = jnp.where(inside, jnp.where(col == row, 1.0, 0.0), blocks[k])
        ahead = [lane(blocks[k], 8 * k + 8 + m) for m in range(8)] if k < 15 else []
        for j in range(0, 8, 2):
            left, right = columns[j], columns[j + 1]
            a, b, d = sub(left, j), sub(right, j), sub(right, j + 1)
            scale = 1.0 / (a * d - b * b)
            a, b, d = a * scale, b * scale, d * scale
            here, there = row == j, row == j + 1
            pair = here | there
            first = jnp.where(here, -d, jnp.where(there, b, left * d - right * b))
            second = jnp.where(here, b, jnp.where(there, -a, right * a - left * b))

            def step(block):
                return jnp.where(pair, 0.0, block) - first * sub(block, j) - second * sub(block, j + 1)

            for m in range(j + 2, 8):
                columns[m] = step(columns[m])
            ahead = [step(block) for block in ahead]
            scaled = step(scaled)
        if k < 15:
            factors = [lane(blocks[k + 1], 8 * k + j) for j in range(8)]
            columns = [
                lane(blocks[k + 1], 8 * k + 8 + m)
                - tree([factors[j] * sub(ahead[m], j) for j in range(8)])
                for m in range(8)
            ]
        rows = [sub(scaled, j) for j in range(8)]
        for i in range(k + 1, 17):
            change = lane(blocks[i], 8 * k) * rows[0]
            for j in range(1, 8):
                change = change + lane(blocks[i], 8 * k + j) * rows[j]
            blocks[i] = jnp.where(inside, change, blocks[i] - change)
    return blocks[16]


def halves(core, own, other):
    is_first = core == 0
    first = jnp.where(is_first, own, other)
    second = jnp.where(is_first, other, own)
    folded = jnp.concatenate([first[:32], second[:32]], axis=0)
    return folded, first[32:33], second[32:33]


def arrivals(source, target, sems, axis):
    copies = []
    for i in range(target.shape[axis] // CHUNK):
        span = pl.ds(i * CHUNK, CHUNK)
        place = (span, slice(None)) if axis == 0 else (slice(None), span)
        copies.append(pltpu.make_async_copy(source.at[place], target.at[place], sems.at[i]))
        copies[-1].start()
    return copies


def chunk_of(i):
    return slice(i * CHUNK, (i + 1) * CHUNK)


def flag(condition, dtype=F32):
    return jnp.where(condition, 1.0, 0.0).astype(dtype)


def first_kernel(
    cells_hbm, cohorts_hbm, x_hbm, y_hbm, x, xt, xt_hbm, out, cells, cohorts, y, x_sems, y_sems, xt_sems, sems
):
    per = CHUNK // WIDTH
    small = [
        pltpu.make_async_copy(cells_hbm, cells, sems.at[0]),
        pltpu.make_async_copy(cohorts_hbm, cohorts, sems.at[1]),
    ]
    for copy in small:
        copy.start()
    x_copies = arrivals(x_hbm, x, x_sems, 0)
    y_copies = arrivals(y_hbm, y, y_sems, 1)
    for copy in small:
        copy.wait()
    group, period = cells[0, 0], cells[0, 1]
    total = jnp.zeros((WIDTH + 16, WIDTH), F32)
    changes = jnp.zeros((1, WIDTH), F32)
    sent = []
    for i, copy in enumerate(x_copies):
        copy.wait()
        here = x[chunk_of(i), :]
        turned = here.T
        xt[:, chunk_of(i)] = turned
        span = pl.ds(i * CHUNK, CHUNK)
        sent.append(pltpu.make_async_copy(xt.at[:, span], xt_hbm.at[:, span], xt_sems.at[i]))
        sent[-1].start()
        left, marks = [], []
        for b in range(per):
            cohort = cohorts[i * per + b]
            treated = flag(cohort == group)
            eligible = treated + flag(cohort > period)
            left.append(turned[:, b * WIDTH : (b + 1) * WIDTH] * eligible.astype(BF16))
            marks.append(jnp.full((16, WIDTH), treated, F32).astype(BF16))
        left = jnp.concatenate([jnp.concatenate(left, axis=1), jnp.concatenate(marks, axis=1)], axis=0)
        total = total + jnp.dot(left, here, preferred_element_type=F32)
    for copy in y_copies:
        copy.wait()
    change = y[pl.ds(period, 1), :] - y[pl.ds(group - 1, 1), :]
    for b in range(cohorts.shape[0]):
        changes = changes + flag(cohorts[b] == group) * change[:, b * WIDTH : (b + 1) * WIDTH]
    folded, diagonal = fold(total[:WIDTH])
    scalar = jnp.sum(changes, axis=1, keepdims=True)
    first_lane = iota((1, WIDTH), 1) == 0
    write_payload(out, folded, (total[WIDTH : WIDTH + 1], jnp.where(first_lane, scalar, diagonal)))
    for copy in sent:
        copy.wait()


def control_kernel(cells, cohorts, x, xt, y, out):
    group, period = cells[0, 0], cells[0, 1]
    per = CHUNK // WIDTH
    total = jnp.zeros((WIDTH + 16, WIDTH), F32)
    for i in range(x.shape[0] // CHUNK):
        span = pl.ds(i * CHUNK, CHUNK)
        change = y[pl.ds(period, 1), span] - y[pl.ds(group - 1, 1), span]
        change = jnp.broadcast_to(change, (16, CHUNK)).astype(BF16)
        turned = jnp.concatenate([xt[:, chunk_of(i)], change], axis=0)
        left = []
        for b in range(per):
            control = flag(cohorts[i * per + b] > period).astype(BF16)
            left.append(turned[:, b * WIDTH : (b + 1) * WIDTH] * control)
        left = jnp.concatenate(left, axis=1)
        total = total + jnp.dot(left, x[chunk_of(i), :], preferred_element_type=F32)
    folded, diagonal = fold(total[:WIDTH])
    out[0:64, :] = folded
    out[64:72, :] = jnp.concatenate(
        [total[WIDTH : WIDTH + 1], diagonal, jnp.zeros((6, WIDTH), F32)], axis=0
    )


def newton_kernel(
    first, cells, cohorts, own, other, x, xt, before, control, coefs, keep, out
):
    group, period = cells[0, 0], cells[0, 1]
    per = CHUNK // WIDTH
    mine = summed(own)
    folded, row, diagonal = halves(lax.axis_index("core"), mine[:40], summed(other)[:40])
    top, low = unfold(folded, diagonal)
    if first:
        keep[...] = jnp.concatenate([row, diagonal, jnp.zeros((6, WIDTH), F32)], axis=0)
        new = 4.0 * solve(top, low, row - 0.5 * top[0:1])
    else:
        keep[...] = mine[32:40]
        new = before[...] + solve(top, low, row)
    coefs[...] = new
    rounded = jnp.concatenate([new, new], axis=0).astype(BF16)
    total = jnp.zeros((WIDTH + 16, WIDTH), F32)
    for i in range(x.shape[0] // CHUNK):
        turned = xt[:, chunk_of(i)]
        index = jnp.dot(rounded, turned, preferred_element_type=F32)[0:8]
        probability = jax.nn.sigmoid(index)
        weight = probability * (1.0 - probability)
        left, errors = [], []
        for b in range(per):
            cohort = cohorts[i * per + b]
            treated = flag(cohort == group)
            eligible = treated + flag(cohort > period)
            span = slice(b * WIDTH, (b + 1) * WIDTH)
            here = jnp.broadcast_to(weight[0:1, span] * eligible, (WIDTH, WIDTH))
            left.append((here * turned[:, span].astype(F32)).astype(BF16))
            error = (treated - probability[:, span]) * eligible
            errors.append(jnp.concatenate([error, error], axis=0).astype(BF16))
        left = jnp.concatenate([jnp.concatenate(left, axis=1), jnp.concatenate(errors, axis=1)], axis=0)
        total = total + jnp.dot(left, x[chunk_of(i), :], preferred_element_type=F32)
    folded, diagonal = fold(total[:WIDTH])
    write_payload(out, folded, (total[WIDTH : WIDTH + 1], diagonal))
    for p in range(out.shape[0]):
        if first:
            out[p, 33:35, :] = control[64:66, :]
            out[p, 40:48, :] = control[8 * p : 8 * p + 8, :]
        else:
            out[p, 40:48, :] = mine[40:48]


def control_solve_kernel(arrived, extras, out):
    folded = jnp.concatenate([arrived[p, 40:48, :] for p in range(arrived.shape[0])], axis=0)
    solved = solve(*unfold(folded, extras[2:3, :]), extras[1:2, :])
    out[...] = solved.astype(BF16).astype(F32)


def last_kernel(cells, own, other, control, before, keep, out):
    folded, row, diagonal = halves(lax.axis_index("core"), summed(own), summed(other))
    new = before[...] + solve(*unfold(folded, diagonal), row)
    ols = control[0:1, :]
    treated_x = keep[0:1, :]
    count = lane(treated_x, 0)
    fitted = jnp.sum(ols * treated_x, axis=1, keepdims=True)
    mean = (lane(keep[1:2, :], 0) - fitted) / count
    out[...] = jnp.concatenate(
        [
            new[0:1].astype(BF16).astype(F32),
            ols,
            mean,
            count,
            jnp.full((1, WIDTH), cells[0, 0].astype(F32), F32),
            jnp.full((1, WIDTH), cells[0, 1].astype(F32), F32),
            jnp.zeros((2, WIDTH), F32),
        ],
        axis=0,
    )


def bring_kernel(message, xt_hbm, y_hbm, mult_hbm, xt, y, mult, xt_sems, y_sems, mult_sems):
    copies = arrivals(xt_hbm, xt, xt_sems, 1) + arrivals(y_hbm, y, y_sems, 1)
    for copy in copies + arrivals(mult_hbm, mult, mult_sems, 0):
        copy.wait()


def draws_kernel(
    cohorts, m0, m1, m2, m3, xt, y, mult, out, treated_out, product_out, odds_out
):
    per = CHUNK // WIDTH
    blank = jnp.zeros((4, WIDTH), F32)

    def stacked(i):
        return jnp.concatenate([m[i : i + 1, :] for m in (m0, m1, m2, m3)] + [blank], axis=0)

    left = jnp.concatenate([stacked(0), stacked(1)], axis=0).astype(BF16)
    mean, count, group, period = stacked(2), stacked(3), stacked(4), stacked(5)
    valid = iota((8, WIDTH), 0) < 4
    per_count = jnp.where(valid, 1.0 / jnp.where(valid, count, 1.0), 0.0)
    group = jnp.where(valid, group, -1.0)
    period = jnp.where(valid, period, 99.0)
    signs = [flag(period == p) - flag(group - 1.0 == p) for p in range(8)]
    total = jnp.zeros((48, WIDTH), F32)
    odds_sum = jnp.zeros((8, WIDTH), F32)
    product_sum = jnp.zeros((8, WIDTH), F32)
    for i in range(xt.shape[1] // CHUNK):
        both = jnp.dot(left, xt[:, chunk_of(i)], preferred_element_type=F32)
        parts = []
        for b in range(per):
            span = slice(b * WIDTH, (b + 1) * WIDTH)
            place = slice(i * CHUNK + b * WIDTH, i * CHUNK + (b + 1) * WIDTH)
            cohort = cohorts[i * per + b].astype(F32)
            outcome = y[:, place]
            change = signs[0] * sub(outcome, 0)
            for p in range(1, 8):
                change = change + signs[p] * sub(outcome, p)
            residual = change - both[8:16, span]
            treated = jnp.where(group == cohort, (residual - mean) * per_count, 0.0)
            odds = jnp.where(period < cohort, jnp.exp(both[0:8, span]), 0.0)
            product = odds * residual
            odds_sum = odds_sum + odds
            product_sum = product_sum + product
            treated_out[:, place] = treated[0:1]
            product_out[:, place] = product[0:1]
            odds_out[:, place] = odds[0:1]
            pairs = []
            for value in (treated, product, odds):
                high = value.astype(BF16).astype(F32)
                pairs.append(jnp.concatenate([high, value - high], axis=0).astype(BF16))
            parts.append(jnp.concatenate(pairs, axis=0))
        total = total + jnp.dot(
            jnp.concatenate(parts, axis=1), mult[chunk_of(i), :], preferred_element_type=F32
        )
    col = iota((8, WIDTH), 1)
    both = jnp.where(
        col == 0,
        jnp.sum(odds_sum, axis=1, keepdims=True),
        jnp.where(col == 1, jnp.sum(product_sum, axis=1, keepdims=True), 0.0),
    )
    rows = [(total[16 * s : 16 * s + 8] + total[16 * s + 8 : 16 * s + 16])[0:4] for s in range(3)]
    rows = jnp.concatenate(rows + [both[0:4]], axis=0)
    for p in range(out.shape[0]):
        out[p] = rows


def relay_kernel(arrived, out):
    rows = out.shape[1]
    total = summed(arrived)[:rows]
    for p in range(out.shape[0]):
        out[p] = total


def finish_kernel(total_rows, arrived, treated, product, odds, influence, bootstrap):
    cell = lax.axis_index("cell")
    sums = summed(arrived)
    weight = lane(sums[12:16], 0)
    mean = lane(sums[12:16], 1) / weight
    draws = math.sqrt(total_rows) * (sums[0:4] - (sums[4:8] - mean * sums[8:12]) / weight)
    for slot in range(4):
        bootstrap[pl.ds(cell ^ slot, 1), :] = draws[slot : slot + 1]
    scale = total_rows / weight[0:1, 0:1]
    influence[...] = total_rows * treated[...] - scale * (product[...] - mean[0:1, 0:1] * odds[...])


def swap_cores(value):
    return lax.ppermute(value, "core", [(0, 1), (1, 0)])


def to_pairs(payload):
    return lax.all_to_all(payload, ("y", "core"), 0, 0)


def to_line(arrived, rows):
    peers = lax.axis_size("z")
    copies = call(relay_kernel, "relay", [shape(peers, rows, WIDTH)], [VMEM])(arrived)
    return lax.all_to_all(copies[0], "z", 0, 0)


def call(kernel, name, outs, ins, out_specs=None, scratch=(), cost=None):
    return pl.pallas_call(
        kernel,
        out_shape=outs,
        in_specs=ins,
        out_specs=out_specs or [VMEM] * len(outs),
        scratch_shapes=list(scratch),
        compiler_params=PARAMS,
        cost_estimate=cost,
        name=name,
    )


def shards(covariates, outcomes, multipliers, cohorts, cells):
    rows_here = covariates.shape[0]
    total_rows = rows_here * lax.axis_size(ROWS)
    pairs = lax.axis_size(("y", "core"))
    sems = pltpu.SemaphoreType.DMA((rows_here // CHUNK,))
    vector = shape(1, rows_here)
    eight = shape(8, WIDTH)
    cost = pl.CostEstimate(flops=1 << 33, bytes_accessed=10 << 20, transcendentals=0)
    tall, wide, wide_hbm, payload = call(
        first_kernel,
        "first",
        [
            shape(rows_here, WIDTH, dtype=BF16),
            shape(WIDTH, rows_here, dtype=BF16),
            pltpu.HBM((WIDTH, rows_here), BF16),
            shape(pairs, 40, WIDTH),
        ],
        [HBM] * 4,
        [FREE, FREE, HBM, VMEM],
        [
            pltpu.SMEM(cells.shape, jnp.int32),
            pltpu.SMEM(cohorts.shape, jnp.int32),
            pltpu.VMEM(outcomes.shape, F32),
            sems,
            sems,
            sems,
            pltpu.SemaphoreType.DMA((2,)),
        ],
    )(*(pltpu.with_memory_space_constraint(v, pltpu.HBM) for v in (cells, cohorts, covariates, outcomes)))
    halfway = to_pairs(payload)
    arrived = to_line(halfway, 40)
    control = call(
        control_kernel, "control", [shape(72, WIDTH)], [SMEM, SMEM, FREE, FREE, FREE], cost=cost
    )(cells, cohorts, tall, wide, outcomes)[0]
    coefs = jnp.zeros((8, WIDTH), F32)
    kept = []
    for step in range(2):
        coefs, keep, payload = call(
            functools.partial(newton_kernel, step == 0),
            "newton",
            [eight, eight, shape(pairs, 48, WIDTH)],
            [SMEM, SMEM, VMEM, VMEM, FREE, FREE, VMEM, VMEM],
        )(cells, cohorts, arrived, swap_cores(arrived), tall, wide, coefs, control)
        kept.append(keep)
        halfway = to_pairs(payload)
        arrived = to_line(halfway, 48 if step == 0 else 40)
    ols = call(control_solve_kernel, "ols", [eight], [VMEM, VMEM], cost=cost)(halfway, kept[1])[0]
    arrived, ols = lax.optimization_barrier((arrived, ols))
    message = call(last_kernel, "last", [eight], [SMEM] + [VMEM] * 5)(
        cells, arrived, swap_cores(arrived), ols, coefs, kept[0]
    )[0]
    wide, deep, mult = call(
        bring_kernel,
        "bring",
        [shape(WIDTH, rows_here, dtype=BF16), shape(*outcomes.shape), shape(rows_here, WIDTH, dtype=BF16)],
        [VMEM] + [HBM] * 3,
        [FREE] * 3,
        [sems, sems, sems],
        cost,
    )(
        message,
        *(pltpu.with_memory_space_constraint(v, pltpu.HBM) for v in (wide_hbm, outcomes, multipliers)),
    )
    messages = [message] + [
        lax.ppermute(message, "cell", [(i, i ^ s) for i in range(4)]) for s in range(1, 4)
    ]
    payload, treated, product, odds = call(
        draws_kernel,
        "draws",
        [shape(pairs, 16, WIDTH), vector, vector, vector],
        [SMEM] + [VMEM] * 4 + [FREE] * 3,
    )(cohorts, *messages, wide, deep, mult)
    arrived = to_line(to_pairs(payload), 16)
    return call(
        functools.partial(finish_kernel, total_rows),
        "finish",
        [vector, shape(4, WIDTH)],
        [VMEM] * 4,
    )(arrived, treated, product, odds)


def solution(mesh):
    fine = Mesh(mesh.devices.reshape(4, 8, 2, 4), ROWS + ("cell",))
    return jax.shard_map(
        shards,
        mesh=fine,
        in_specs=(P(ROWS, None), P(None, ROWS), P(ROWS, "cell"), P(ROWS), P("cell", None)),
        out_specs=(P("cell", ROWS), P(None, "cell")),
        check_vma=False,
    )
```

```python
import functools
import math

import jax
import jax.numpy as jnp
from jax import lax
from jax.experimental import pallas as pl
from jax.experimental.pallas import tpu as pltpu
from jax.sharding import Mesh, PartitionSpec as P

ROWS = ("y", "z", "core")
F32 = jnp.float32
BF16 = jnp.bfloat16
WIDTH = 128
HALF = 64
CHUNK = 4096
PACKED = 40
VMEM = pl.BlockSpec(memory_space=pltpu.VMEM)
SMEM = pl.BlockSpec(memory_space=pltpu.SMEM)
HBM = pl.BlockSpec(memory_space=pltpu.HBM)
FREE = pl.BlockSpec()
PARAMS = pltpu.CompilerParams(vmem_limit_bytes=24 << 20)


def shape(*dims, dtype=F32):
    return jax.ShapeDtypeStruct(dims, dtype)


def iota(dims, axis):
    return lax.broadcasted_iota(jnp.int32, dims, axis)


def fold(gram):
    top, low = gram[:HALF], gram[HALF:]
    row, col = iota((HALF, WIDTH), 0), iota((HALF, WIDTH), 1)
    folded = jnp.where((col < HALF) & (col > row), pltpu.roll(low, HALF, 1), top)
    diagonal = jnp.sum(jnp.where(col - HALF == row, low, 0.0), axis=0, keepdims=True)
    return folded, diagonal


def unfold(folded, diagonal):
    row, col = iota((HALF, WIDTH), 0), iota((HALF, WIDTH), 1)
    turned = jnp.concatenate([folded, jnp.zeros_like(folded)], axis=0).T
    top = jnp.where((col >= HALF) | (col <= row), folded, turned[:HALF])
    right = col - HALF
    low = jnp.where(
        right > row,
        pltpu.roll(folded, HALF, 1),
        jnp.where(right < row, pltpu.roll(turned[:HALF], HALF, 1), diagonal),
    )
    return top, jnp.where(col < HALF, turned[HALF:], low)


def write_payload(out, folded, extras):
    pad = jnp.zeros((7, WIDTH), F32)
    for p in range(out.shape[0]):
        h = p % 2
        out[p, 0:32, :] = folded[32 * h : 32 * h + 32]
        out[p, 32:40, :] = jnp.concatenate([extras[h], pad], axis=0)


def summed(ref):
    total = ref[0]
    for p in range(1, ref.shape[0]):
        total = total + ref[p]
    return total


def lane(block, i):
    return jnp.broadcast_to(block[:, i : i + 1], block.shape)


def sub(block, i):
    return jnp.broadcast_to(block[i : i + 1, :], block.shape)


def tree(terms):
    while len(terms) > 1:
        terms = [terms[i] + terms[i + 1] for i in range(0, len(terms), 2)]
    return terms[0]


def solve(top, low, vector):
    blocks = [top[8 * i : 8 * i + 8] for i in range(8)] + [low[8 * i : 8 * i + 8] for i in range(8)]
    blocks.append(jnp.broadcast_to(vector, (8, WIDTH)))
    row = iota((8, WIDTH), 0)
    columns = [lane(blocks[0], m) for m in range(8)]
    for k in range(16):
        col = iota((8, WIDTH), 1) - 8 * k
        inside = (col >= 0) & (col < 8)
        scaled = jnp.where(inside, jnp.where(col == row, 1.0, 0.0), blocks[k])
        ahead = [lane(blocks[k], 8 * k + 8 + m) for m in range(8)] if k < 15 else []
        for j in range(0, 8, 2):
            left, right = columns[j], columns[j + 1]
            a, b, d = sub(left, j), sub(right, j), sub(right, j + 1)
            scale = 1.0 / (a * d - b * b)
            a, b, d = a * scale, b * scale, d * scale
            here, there = row == j, row == j + 1
            pair = here | there
            first = jnp.where(here, -d, jnp.where(there, b, left * d - right * b))
            second = jnp.where(here, b, jnp.where(there, -a, right * a - left * b))

            def step(block):
                return jnp.where(pair, 0.0, block) - first * sub(block, j) - second * sub(block, j + 1)

            for m in range(j + 2, 8):
                columns[m] = step(columns[m])
            ahead = [step(block) for block in ahead]
            scaled = step(scaled)
        if k < 15:
            factors = [lane(blocks[k + 1], 8 * k + j) for j in range(8)]
            columns = [
                lane(blocks[k + 1], 8 * k + 8 + m)
                - tree([factors[j] * sub(ahead[m], j) for j in range(8)])
                for m in range(8)
            ]
        rows = [sub(scaled, j) for j in range(8)]
        for i in range(k + 1, 17):
            change = lane(blocks[i], 8 * k) * rows[0]
            for j in range(1, 8):
                change = change + lane(blocks[i], 8 * k + j) * rows[j]
            blocks[i] = jnp.where(inside, change, blocks[i] - change)
    return blocks[16]


def halves(core, own, other):
    is_first = core == 0
    first = jnp.where(is_first, own, other)
    second = jnp.where(is_first, other, own)
    folded = jnp.concatenate([first[:32], second[:32]], axis=0)
    return folded, first[32:33], second[32:33]


def arrivals(source, target, sems, axis):
    copies = []
    for i in range(target.shape[axis] // CHUNK):
        span = pl.ds(i * CHUNK, CHUNK)
        place = (span, slice(None)) if axis == 0 else (slice(None), span)
        copies.append(pltpu.make_async_copy(source.at[place], target.at[place], sems.at[i]))
        copies[-1].start()
    return copies


def chunk_of(i):
    return slice(i * CHUNK, (i + 1) * CHUNK)


def flag(condition, dtype=F32):
    return jnp.where(condition, 1.0, 0.0).astype(dtype)


def first_kernel(
    cells_hbm, cohorts_hbm, x_hbm, y_hbm, x, xt, out, cells, cohorts, y, x_sems, y_sems, sems
):
    per = CHUNK // WIDTH
    small = [
        pltpu.make_async_copy(cells_hbm, cells, sems.at[0]),
        pltpu.make_async_copy(cohorts_hbm, cohorts, sems.at[1]),
    ]
    for copy in small:
        copy.start()
    x_copies = arrivals(x_hbm, x, x_sems, 0)
    y_copies = arrivals(y_hbm, y, y_sems, 1)
    for copy in small:
        copy.wait()
    group, period = cells[0, 0], cells[0, 1]
    total = jnp.zeros((WIDTH + 16, WIDTH), F32)
    changes = jnp.zeros((1, WIDTH), F32)
    for i, copy in enumerate(x_copies):
        copy.wait()
        here = x[chunk_of(i), :]
        turned = here.T
        xt[:, chunk_of(i)] = turned
        left, marks = [], []
        for b in range(per):
            cohort = cohorts[i * per + b]
            treated = flag(cohort == group)
            eligible = treated + flag(cohort > period)
            left.append(turned[:, b * WIDTH : (b + 1) * WIDTH] * eligible.astype(BF16))
            marks.append(jnp.full((16, WIDTH), treated, F32).astype(BF16))
        left = jnp.concatenate([jnp.concatenate(left, axis=1), jnp.concatenate(marks, axis=1)], axis=0)
        total = total + jnp.dot(left, here, preferred_element_type=F32)
    for copy in y_copies:
        copy.wait()
    change = y[pl.ds(period, 1), :] - y[pl.ds(group - 1, 1), :]
    for b in range(cohorts.shape[0]):
        changes = changes + flag(cohorts[b] == group) * change[:, b * WIDTH : (b + 1) * WIDTH]
    folded, diagonal = fold(total[:WIDTH])
    scalar = jnp.sum(changes, axis=1, keepdims=True)
    first_lane = iota((1, WIDTH), 1) == 0
    write_payload(out, folded, (total[WIDTH : WIDTH + 1], jnp.where(first_lane, scalar, diagonal)))


def control_kernel(cells, cohorts, x, xt, y, out):
    group, period = cells[0, 0], cells[0, 1]
    per = CHUNK // WIDTH
    total = jnp.zeros((WIDTH + 16, WIDTH), F32)
    for i in range(x.shape[0] // CHUNK):
        span = pl.ds(i * CHUNK, CHUNK)
        change = y[pl.ds(period, 1), span] - y[pl.ds(group - 1, 1), span]
        change = jnp.broadcast_to(change, (16, CHUNK)).astype(BF16)
        turned = jnp.concatenate([xt[:, chunk_of(i)], change], axis=0)
        left = []
        for b in range(per):
            control = flag(cohorts[i * per + b] > period).astype(BF16)
            left.append(turned[:, b * WIDTH : (b + 1) * WIDTH] * control)
        left = jnp.concatenate(left, axis=1)
        total = total + jnp.dot(left, x[chunk_of(i), :], preferred_element_type=F32)
    folded, diagonal = fold(total[:WIDTH])
    out[0:64, :] = folded
    out[64:72, :] = jnp.concatenate(
        [total[WIDTH : WIDTH + 1], diagonal, jnp.zeros((6, WIDTH), F32)], axis=0
    )


def newton_kernel(
    first, cells, cohorts, own, other, x, xt, before, control, coefs, keep, out
):
    group, period = cells[0, 0], cells[0, 1]
    per = CHUNK // WIDTH
    mine = summed(own)
    folded, row, diagonal = halves(lax.axis_index("core"), mine[:40], summed(other)[:40])
    top, low = unfold(folded, diagonal)
    if first:
        keep[...] = jnp.concatenate([row, diagonal, jnp.zeros((6, WIDTH), F32)], axis=0)
        new = 4.0 * solve(top, low, row - 0.5 * top[0:1])
    else:
        keep[...] = mine[32:40]
        new = before[...] + solve(top, low, row)
    coefs[...] = new
    rounded = jnp.concatenate([new, new], axis=0).astype(BF16)
    total = jnp.zeros((WIDTH + 16, WIDTH), F32)
    for i in range(x.shape[0] // CHUNK):
        turned = xt[:, chunk_of(i)]
        index = jnp.dot(rounded, turned, preferred_element_type=F32)[0:8]
        probability = jax.nn.sigmoid(index)
        weight = probability * (1.0 - probability)
        left, errors = [], []
        for b in range(per):
            cohort = cohorts[i * per + b]
            treated = flag(cohort == group)
            eligible = treated + flag(cohort > period)
            span = slice(b * WIDTH, (b + 1) * WIDTH)
            here = jnp.broadcast_to(weight[0:1, span] * eligible, (WIDTH, WIDTH))
            left.append((here * turned[:, span].astype(F32)).astype(BF16))
            error = (treated - probability[:, span]) * eligible
            errors.append(jnp.concatenate([error, error], axis=0).astype(BF16))
        left = jnp.concatenate([jnp.concatenate(left, axis=1), jnp.concatenate(errors, axis=1)], axis=0)
        total = total + jnp.dot(left, x[chunk_of(i), :], preferred_element_type=F32)
    folded, diagonal = fold(total[:WIDTH])
    write_payload(out, folded, (total[WIDTH : WIDTH + 1], diagonal))
    for p in range(out.shape[0]):
        if first:
            out[p, 33:35, :] = control[64:66, :]
            out[p, 40:48, :] = control[8 * p : 8 * p + 8, :]
        else:
            out[p, 40:48, :] = mine[40:48]


def control_solve_kernel(arrived, extras, out):
    folded = jnp.concatenate([arrived[p, 40:48, :] for p in range(arrived.shape[0])], axis=0)
    solved = solve(*unfold(folded, extras[2:3, :]), extras[1:2, :])
    out[...] = solved.astype(BF16).astype(F32)


def last_kernel(cells, own, other, control, before, keep, out):
    folded, row, diagonal = halves(lax.axis_index("core"), summed(own), summed(other))
    new = before[...] + solve(*unfold(folded, diagonal), row)
    ols = control[0:1, :]
    treated_x = keep[0:1, :]
    count = lane(treated_x, 0)
    fitted = jnp.sum(ols * treated_x, axis=1, keepdims=True)
    mean = (lane(keep[1:2, :], 0) - fitted) / count
    out[...] = jnp.concatenate(
        [
            new[0:1].astype(BF16).astype(F32),
            ols,
            mean,
            count,
            jnp.full((1, WIDTH), cells[0, 0].astype(F32), F32),
            jnp.full((1, WIDTH), cells[0, 1].astype(F32), F32),
            jnp.zeros((2, WIDTH), F32),
        ],
        axis=0,
    )


def bring_kernel(message, x_hbm, y_hbm, mult_hbm, x, y, mult, x_sems, y_sems, mult_sems):
    copies = arrivals(x_hbm, x, x_sems, 0) + arrivals(y_hbm, y, y_sems, 1)
    for copy in copies + arrivals(mult_hbm, mult, mult_sems, 0):
        copy.wait()


def draws_kernel(
    cohorts, m0, m1, m2, m3, x, y, mult, out, treated_out, product_out, odds_out
):
    per = CHUNK // WIDTH
    blank = jnp.zeros((4, WIDTH), F32)

    def stacked(i):
        return jnp.concatenate([m[i : i + 1, :] for m in (m0, m1, m2, m3)] + [blank], axis=0)

    left = jnp.concatenate([stacked(0), stacked(1)], axis=0).astype(BF16)
    mean, count, group, period = stacked(2), stacked(3), stacked(4), stacked(5)
    valid = iota((8, WIDTH), 0) < 4
    per_count = jnp.where(valid, 1.0 / jnp.where(valid, count, 1.0), 0.0)
    group = jnp.where(valid, group, -1.0)
    period = jnp.where(valid, period, 99.0)
    signs = [flag(period == p) - flag(group - 1.0 == p) for p in range(8)]
    total = jnp.zeros((48, WIDTH), F32)
    odds_sum = jnp.zeros((8, WIDTH), F32)
    product_sum = jnp.zeros((8, WIDTH), F32)
    for i in range(x.shape[0] // CHUNK):
        both = lax.dot_general(
            left, x[chunk_of(i), :], (((1,), (1,)), ((), ())), preferred_element_type=F32
        )
        parts = []
        for b in range(per):
            span = slice(b * WIDTH, (b + 1) * WIDTH)
            place = slice(i * CHUNK + b * WIDTH, i * CHUNK + (b + 1) * WIDTH)
            cohort = cohorts[i * per + b].astype(F32)
            outcome = y[:, place]
            change = signs[0] * sub(outcome, 0)
            for p in range(1, 8):
                change = change + signs[p] * sub(outcome, p)
            residual = change - both[8:16, span]
            treated = jnp.where(group == cohort, (residual - mean) * per_count, 0.0)
            odds = jnp.where(period < cohort, jnp.exp(both[0:8, span]), 0.0)
            product = odds * residual
            odds_sum = odds_sum + odds
            product_sum = product_sum + product
            treated_out[:, place] = treated[0:1]
            product_out[:, place] = product[0:1]
            odds_out[:, place] = odds[0:1]
            pairs = []
            for value in (treated, product, odds):
                high = value.astype(BF16).astype(F32)
                pairs.append(jnp.concatenate([high, value - high], axis=0).astype(BF16))
            parts.append(jnp.concatenate(pairs, axis=0))
        total = total + jnp.dot(
            jnp.concatenate(parts, axis=1), mult[chunk_of(i), :], preferred_element_type=F32
        )
    col = iota((8, WIDTH), 1)
    both = jnp.where(
        col == 0,
        jnp.sum(odds_sum, axis=1, keepdims=True),
        jnp.where(col == 1, jnp.sum(product_sum, axis=1, keepdims=True), 0.0),
    )
    rows = [(total[16 * s : 16 * s + 8] + total[16 * s + 8 : 16 * s + 16])[0:4] for s in range(3)]
    rows = jnp.concatenate(rows + [both[0:4]], axis=0)
    for p in range(out.shape[0]):
        out[p] = rows


def relay_kernel(arrived, out):
    rows = out.shape[1]
    total = summed(arrived)[:rows]
    for p in range(out.shape[0]):
        out[p] = total


def finish_kernel(total_rows, arrived, treated, product, odds, influence, bootstrap):
    cell = lax.axis_index("cell")
    sums = summed(arrived)
    weight = lane(sums[12:16], 0)
    mean = lane(sums[12:16], 1) / weight
    draws = math.sqrt(total_rows) * (sums[0:4] - (sums[4:8] - mean * sums[8:12]) / weight)
    for slot in range(4):
        bootstrap[pl.ds(cell ^ slot, 1), :] = draws[slot : slot + 1]
    scale = total_rows / weight[0:1, 0:1]
    influence[...] = total_rows * treated[...] - scale * (product[...] - mean[0:1, 0:1] * odds[...])


def swap_cores(value):
    return lax.ppermute(value, "core", [(0, 1), (1, 0)])


def to_pairs(payload):
    return lax.all_to_all(payload, ("y", "core"), 0, 0)


def to_line(arrived, rows):
    peers = lax.axis_size("z")
    copies = call(relay_kernel, "relay", [shape(peers, rows, WIDTH)], [VMEM])(arrived)
    return lax.all_to_all(copies[0], "z", 0, 0)


def call(kernel, name, outs, ins, out_specs=None, scratch=(), cost=None):
    return pl.pallas_call(
        kernel,
        out_shape=outs,
        in_specs=ins,
        out_specs=out_specs or [VMEM] * len(outs),
        scratch_shapes=list(scratch),
        compiler_params=PARAMS,
        cost_estimate=cost,
        name=name,
    )


def shards(covariates, outcomes, multipliers, cohorts, cells):
    rows_here = covariates.shape[0]
    total_rows = rows_here * lax.axis_size(ROWS)
    pairs = lax.axis_size(("y", "core"))
    sems = pltpu.SemaphoreType.DMA((rows_here // CHUNK,))
    vector = shape(1, rows_here)
    eight = shape(8, WIDTH)
    cost = pl.CostEstimate(flops=1 << 33, bytes_accessed=10 << 20, transcendentals=0)
    tall, wide, payload = call(
        first_kernel,
        "first",
        [
            shape(rows_here, WIDTH, dtype=BF16),
            shape(WIDTH, rows_here, dtype=BF16),
            shape(pairs, 40, WIDTH),
        ],
        [HBM] * 4,
        [FREE, FREE, VMEM],
        [
            pltpu.SMEM(cells.shape, jnp.int32),
            pltpu.SMEM(cohorts.shape, jnp.int32),
            pltpu.VMEM(outcomes.shape, F32),
            sems,
            sems,
            pltpu.SemaphoreType.DMA((2,)),
        ],
    )(*(pltpu.with_memory_space_constraint(v, pltpu.HBM) for v in (cells, cohorts, covariates, outcomes)))
    halfway = to_pairs(payload)
    arrived = to_line(halfway, 40)
    control = call(
        control_kernel, "control", [shape(72, WIDTH)], [SMEM, SMEM, FREE, FREE, FREE], cost=cost
    )(cells, cohorts, tall, wide, outcomes)[0]
    coefs = jnp.zeros((8, WIDTH), F32)
    kept = []
    for step in range(2):
        coefs, keep, payload = call(
            functools.partial(newton_kernel, step == 0),
            "newton",
            [eight, eight, shape(pairs, 48, WIDTH)],
            [SMEM, SMEM, VMEM, VMEM, FREE, FREE, VMEM, VMEM],
        )(cells, cohorts, arrived, swap_cores(arrived), tall, wide, coefs, control)
        kept.append(keep)
        halfway = to_pairs(payload)
        arrived = to_line(halfway, 48 if step == 0 else 40)
    ols = call(control_solve_kernel, "ols", [eight], [VMEM, VMEM], cost=cost)(halfway, kept[1])[0]
    arrived, ols = lax.optimization_barrier((arrived, ols))
    message = call(last_kernel, "last", [eight], [SMEM] + [VMEM] * 5)(
        cells, arrived, swap_cores(arrived), ols, coefs, kept[0]
    )[0]
    near, deep, mult = call(
        bring_kernel,
        "bring",
        [shape(rows_here, WIDTH, dtype=BF16), shape(*outcomes.shape), shape(rows_here, WIDTH, dtype=BF16)],
        [VMEM] + [HBM] * 3,
        [FREE] * 3,
        [sems, sems, sems],
        cost,
    )(
        message,
        *(pltpu.with_memory_space_constraint(v, pltpu.HBM) for v in (covariates, outcomes, multipliers)),
    )
    messages = [message] + [
        lax.ppermute(message, "cell", [(i, i ^ s) for i in range(4)]) for s in range(1, 4)
    ]
    payload, treated, product, odds = call(
        draws_kernel,
        "draws",
        [shape(pairs, 16, WIDTH), vector, vector, vector],
        [SMEM] + [VMEM] * 4 + [FREE] * 3,
    )(cohorts, *messages, near, deep, mult)
    arrived = to_line(to_pairs(payload), 16)
    return call(
        functools.partial(finish_kernel, total_rows),
        "finish",
        [vector, shape(4, WIDTH)],
        [VMEM] * 4,
    )(arrived, treated, product, odds)


def solution(mesh):
    fine = Mesh(mesh.devices.reshape(4, 8, 2, 4), ROWS + ("cell",))
    return jax.shard_map(
        shards,
        mesh=fine,
        in_specs=(P(ROWS, None), P(None, ROWS), P(ROWS, "cell"), P(ROWS), P("cell", None)),
        out_specs=(P("cell", ROWS), P(None, "cell")),
        check_vma=False,
    )
```

```python
import functools
import math

import jax
import jax.numpy as jnp
from jax import lax
from jax.experimental import pallas as pl
from jax.experimental.pallas import tpu as pltpu
from jax.sharding import Mesh, PartitionSpec as P

ROWS = ("y", "z", "core")
F32 = jnp.float32
BF16 = jnp.bfloat16
WIDTH = 128
HALF = 64
CHUNK = 4096
VMEM = pl.BlockSpec(memory_space=pltpu.VMEM)
SMEM = pl.BlockSpec(memory_space=pltpu.SMEM)
HBM = pl.BlockSpec(memory_space=pltpu.HBM)
FREE = pl.BlockSpec()
PARAMS = pltpu.CompilerParams(vmem_limit_bytes=24 << 20)


def shape(*dims, dtype=F32):
    return jax.ShapeDtypeStruct(dims, dtype)


def iota(dims, axis):
    return lax.broadcasted_iota(jnp.int32, dims, axis)


def fold(gram):
    top, low = gram[:HALF], gram[HALF:]
    row, col = iota((HALF, WIDTH), 0), iota((HALF, WIDTH), 1)
    folded = jnp.where((col < HALF) & (col > row), pltpu.roll(low, HALF, 1), top)
    diagonal = jnp.sum(jnp.where(col - HALF == row, low, 0.0), axis=0, keepdims=True)
    return folded, diagonal


def unfold(folded, diagonal):
    row, col = iota((HALF, WIDTH), 0), iota((HALF, WIDTH), 1)
    turned = jnp.concatenate([folded, jnp.zeros_like(folded)], axis=0).T
    top = jnp.where((col >= HALF) | (col <= row), folded, turned[:HALF])
    right = col - HALF
    low = jnp.where(
        right > row,
        pltpu.roll(folded, HALF, 1),
        jnp.where(right < row, pltpu.roll(turned[:HALF], HALF, 1), diagonal),
    )
    return top, jnp.where(col < HALF, turned[HALF:], low)


def packed(rows):
    spots = [(i, i + 17) for i in range(17)] + [(i, i + 5) for i in range(34, rows.shape[0] - 5)]
    return jnp.concatenate(
        [jnp.concatenate([rows[i : i + 1], rows[j : j + 1]], axis=0) for i, j in spots], axis=1
    )


def unpacked(value, first, count):
    rows = []
    for i in range(first, first + count):
        part, spot = divmod(i, 17) if i < 34 else divmod(i - 34, 5)
        spot = spot + 17 if i >= 34 else spot
        rows.append(value[part : part + 1, spot * WIDTH : (spot + 1) * WIDTH])
    return jnp.concatenate(rows, axis=0)


def write_payload(out, folded, extras, more=None):
    for p in range(out.shape[0]):
        h = p % 2
        rows = [folded[32 * h : 32 * h + 32], extras[h], jnp.zeros((1, WIDTH), F32)]
        rows += [more[p]] if more else []
        out[p] = packed(jnp.concatenate(rows, axis=0))


def summed(ref):
    total = ref[0]
    for p in range(1, ref.shape[0]):
        total = total + ref[p]
    return total


def lane(block, i):
    return jnp.broadcast_to(block[:, i : i + 1], block.shape)


def sub(block, i):
    return jnp.broadcast_to(block[i : i + 1, :], block.shape)


def tree(terms):
    while len(terms) > 1:
        terms = [terms[i] + terms[i + 1] for i in range(0, len(terms), 2)]
    return terms[0]


def solve(top, low, vector):
    blocks = [top[8 * i : 8 * i + 8] for i in range(8)] + [low[8 * i : 8 * i + 8] for i in range(8)]
    blocks.append(jnp.broadcast_to(vector, (8, WIDTH)))
    row = iota((8, WIDTH), 0)
    columns = [lane(blocks[0], m) for m in range(8)]
    for k in range(16):
        col = iota((8, WIDTH), 1) - 8 * k
        inside = (col >= 0) & (col < 8)
        scaled = jnp.where(inside, jnp.where(col == row, 1.0, 0.0), blocks[k])
        ahead = [lane(blocks[k], 8 * k + 8 + m) for m in range(8)] if k < 15 else []
        for j in range(0, 8, 2):
            left, right = columns[j], columns[j + 1]
            a, b, d = sub(left, j), sub(right, j), sub(right, j + 1)
            scale = 1.0 / (a * d - b * b)
            a, b, d = a * scale, b * scale, d * scale
            here, there = row == j, row == j + 1
            pair = here | there
            first = jnp.where(here, -d, jnp.where(there, b, left * d - right * b))
            second = jnp.where(here, b, jnp.where(there, -a, right * a - left * b))

            def step(block):
                return jnp.where(pair, 0.0, block) - first * sub(block, j) - second * sub(block, j + 1)

            for m in range(j + 2, 8):
                columns[m] = step(columns[m])
            ahead = [step(block) for block in ahead]
            scaled = step(scaled)
        if k < 15:
            factors = [lane(blocks[k + 1], 8 * k + j) for j in range(8)]
            columns = [
                lane(blocks[k + 1], 8 * k + 8 + m)
                - tree([factors[j] * sub(ahead[m], j) for j in range(8)])
                for m in range(8)
            ]
        rows = [sub(scaled, j) for j in range(8)]
        for i in range(k + 1, 17):
            change = lane(blocks[i], 8 * k) * rows[0]
            for j in range(1, 8):
                change = change + lane(blocks[i], 8 * k + j) * rows[j]
            blocks[i] = jnp.where(inside, change, blocks[i] - change)
    return blocks[16]


def halves(core, own, other):
    is_first = core == 0
    first = jnp.where(is_first, own, other)
    second = jnp.where(is_first, other, own)
    folded = jnp.concatenate([first[:32], second[:32]], axis=0)
    return folded, first[32:33], second[32:33]


def arrivals(source, target, sems, axis):
    copies = []
    for i in range(target.shape[axis] // CHUNK):
        span = pl.ds(i * CHUNK, CHUNK)
        place = (span, slice(None)) if axis == 0 else (slice(None), span)
        copies.append(pltpu.make_async_copy(source.at[place], target.at[place], sems.at[i]))
        copies[-1].start()
    return copies


def chunk_of(i):
    return slice(i * CHUNK, (i + 1) * CHUNK)


def flag(condition, dtype=F32):
    return jnp.where(condition, 1.0, 0.0).astype(dtype)


def first_kernel(
    cells_hbm, cohorts_hbm, x_hbm, y_hbm, x, xt, out, cells, cohorts, y, x_sems, y_sems, sems
):
    per = CHUNK // WIDTH
    small = [
        pltpu.make_async_copy(cells_hbm, cells, sems.at[0]),
        pltpu.make_async_copy(cohorts_hbm, cohorts, sems.at[1]),
    ]
    for copy in small:
        copy.start()
    x_copies = arrivals(x_hbm, x, x_sems, 0)
    y_copies = arrivals(y_hbm, y, y_sems, 1)
    for copy in small:
        copy.wait()
    group, period = cells[0, 0], cells[0, 1]
    total = jnp.zeros((WIDTH + 16, WIDTH), F32)
    changes = jnp.zeros((1, WIDTH), F32)
    for i, copy in enumerate(x_copies):
        copy.wait()
        here = x[chunk_of(i), :]
        turned = here.T
        xt[:, chunk_of(i)] = turned
        left, marks = [], []
        for b in range(per):
            cohort = cohorts[i * per + b]
            treated = flag(cohort == group)
            eligible = treated + flag(cohort > period)
            left.append(turned[:, b * WIDTH : (b + 1) * WIDTH] * eligible.astype(BF16))
            marks.append(jnp.full((16, WIDTH), treated, F32).astype(BF16))
        left = jnp.concatenate([jnp.concatenate(left, axis=1), jnp.concatenate(marks, axis=1)], axis=0)
        total = total + jnp.dot(left, here, preferred_element_type=F32)
    for copy in y_copies:
        copy.wait()
    change = y[pl.ds(period, 1), :] - y[pl.ds(group - 1, 1), :]
    for b in range(cohorts.shape[0]):
        changes = changes + flag(cohorts[b] == group) * change[:, b * WIDTH : (b + 1) * WIDTH]
    folded, diagonal = fold(total[:WIDTH])
    scalar = jnp.sum(changes, axis=1, keepdims=True)
    first_lane = iota((1, WIDTH), 1) == 0
    write_payload(out, folded, (total[WIDTH : WIDTH + 1], jnp.where(first_lane, scalar, diagonal)))


def control_kernel(cells, cohorts, x, xt, y, out):
    group, period = cells[0, 0], cells[0, 1]
    per = CHUNK // WIDTH
    total = jnp.zeros((WIDTH + 16, WIDTH), F32)
    for i in range(x.shape[0] // CHUNK):
        span = pl.ds(i * CHUNK, CHUNK)
        change = y[pl.ds(period, 1), span] - y[pl.ds(group - 1, 1), span]
        change = jnp.broadcast_to(change, (16, CHUNK)).astype(BF16)
        turned = jnp.concatenate([xt[:, chunk_of(i)], change], axis=0)
        left = []
        for b in range(per):
            control = flag(cohorts[i * per + b] > period).astype(BF16)
            left.append(turned[:, b * WIDTH : (b + 1) * WIDTH] * control)
        left = jnp.concatenate(left, axis=1)
        total = total + jnp.dot(left, x[chunk_of(i), :], preferred_element_type=F32)
    folded, diagonal = fold(total[:WIDTH])
    out[0:64, :] = folded
    out[64:72, :] = jnp.concatenate(
        [total[WIDTH : WIDTH + 1], diagonal, jnp.zeros((6, WIDTH), F32)], axis=0
    )


def newton_kernel(
    first, cells, cohorts, own, other, x, xt, before, control, coefs, keep, out
):
    group, period = cells[0, 0], cells[0, 1]
    per = CHUNK // WIDTH
    mine = summed(own)
    core = lax.axis_index("core")
    folded, row, diagonal = halves(core, unpacked(mine, 0, 33), unpacked(summed(other), 0, 33))
    top, low = unfold(folded, diagonal)
    if first:
        keep[...] = jnp.concatenate([row, diagonal, jnp.zeros((6, WIDTH), F32)], axis=0)
        new = 4.0 * solve(top, low, row - 0.5 * top[0:1])
    else:
        keep[...] = jnp.concatenate([unpacked(mine, 34, 2), jnp.zeros((6, WIDTH), F32)], axis=0)
        new = before[...] + solve(top, low, row)
    coefs[...] = new
    rounded = jnp.concatenate([new, new], axis=0).astype(BF16)
    total = jnp.zeros((WIDTH + 16, WIDTH), F32)
    for i in range(x.shape[0] // CHUNK):
        turned = xt[:, chunk_of(i)]
        index = jnp.dot(rounded, turned, preferred_element_type=F32)[0:8]
        probability = jax.nn.sigmoid(index)
        weight = probability * (1.0 - probability)
        left, errors = [], []
        for b in range(per):
            cohort = cohorts[i * per + b]
            treated = flag(cohort == group)
            eligible = treated + flag(cohort > period)
            span = slice(b * WIDTH, (b + 1) * WIDTH)
            here = jnp.broadcast_to(weight[0:1, span] * eligible, (WIDTH, WIDTH))
            left.append((here * turned[:, span].astype(F32)).astype(BF16))
            error = (treated - probability[:, span]) * eligible
            errors.append(jnp.concatenate([error, error], axis=0).astype(BF16))
        left = jnp.concatenate([jnp.concatenate(left, axis=1), jnp.concatenate(errors, axis=1)], axis=0)
        total = total + jnp.dot(left, x[chunk_of(i), :], preferred_element_type=F32)
    folded, diagonal = fold(total[:WIDTH])
    if first:
        more = [
            jnp.concatenate([control[64:66, :], control[8 * p : 8 * p + 8, :]], axis=0)
            for p in range(out.shape[0])
        ]
    else:
        piece = jnp.concatenate([jnp.zeros((2, WIDTH), F32), unpacked(mine, 36, 8)], axis=0)
        more = [piece] * out.shape[0]
    write_payload(out, folded, (total[WIDTH : WIDTH + 1], diagonal), more)


def control_solve_kernel(arrived, extras, out):
    folded = jnp.concatenate([unpacked(arrived[p], 36, 8) for p in range(arrived.shape[0])], axis=0)
    solved = solve(*unfold(folded, extras[1:2, :]), extras[0:1, :])
    out[...] = solved.astype(BF16).astype(F32)


def last_kernel(cells, own, other, control, before, keep, out):
    core = lax.axis_index("core")
    folded, row, diagonal = halves(core, unpacked(summed(own), 0, 33), unpacked(summed(other), 0, 33))
    new = before[...] + solve(*unfold(folded, diagonal), row)
    ols = control[0:1, :]
    treated_x = keep[0:1, :]
    count = lane(treated_x, 0)
    fitted = jnp.sum(ols * treated_x, axis=1, keepdims=True)
    mean = (lane(keep[1:2, :], 0) - fitted) / count
    out[...] = jnp.concatenate(
        [
            new[0:1].astype(BF16).astype(F32),
            ols,
            mean,
            count,
            jnp.full((1, WIDTH), cells[0, 0].astype(F32), F32),
            jnp.full((1, WIDTH), cells[0, 1].astype(F32), F32),
            jnp.zeros((2, WIDTH), F32),
        ],
        axis=0,
    )


def bring_kernel(message, x_hbm, y_hbm, mult_hbm, x, y, mult, x_sems, y_sems, mult_sems):
    copies = arrivals(x_hbm, x, x_sems, 0) + arrivals(y_hbm, y, y_sems, 1)
    for copy in copies + arrivals(mult_hbm, mult, mult_sems, 0):
        copy.wait()


def draws_kernel(
    cohorts, m0, m1, m2, m3, x, y, mult, out, treated_out, product_out, odds_out
):
    per = CHUNK // WIDTH
    blank = jnp.zeros((4, WIDTH), F32)

    def stacked(i):
        return jnp.concatenate([m[i : i + 1, :] for m in (m0, m1, m2, m3)] + [blank], axis=0)

    left = jnp.concatenate([stacked(0), stacked(1)], axis=0).astype(BF16)
    mean, count, group, period = stacked(2), stacked(3), stacked(4), stacked(5)
    valid = iota((8, WIDTH), 0) < 4
    per_count = jnp.where(valid, 1.0 / jnp.where(valid, count, 1.0), 0.0)
    group = jnp.where(valid, group, -1.0)
    period = jnp.where(valid, period, 99.0)
    signs = [flag(period == p) - flag(group - 1.0 == p) for p in range(8)]
    total = jnp.zeros((48, WIDTH), F32)
    odds_sum = jnp.zeros((8, WIDTH), F32)
    product_sum = jnp.zeros((8, WIDTH), F32)
    for i in range(x.shape[0] // CHUNK):
        both = lax.dot_general(
            left, x[chunk_of(i), :], (((1,), (1,)), ((), ())), preferred_element_type=F32
        )
        parts = []
        for b in range(per):
            span = slice(b * WIDTH, (b + 1) * WIDTH)
            place = slice(i * CHUNK + b * WIDTH, i * CHUNK + (b + 1) * WIDTH)
            cohort = cohorts[i * per + b].astype(F32)
            outcome = y[:, place]
            change = signs[0] * sub(outcome, 0)
            for p in range(1, 8):
                change = change + signs[p] * sub(outcome, p)
            residual = change - both[8:16, span]
            treated = jnp.where(group == cohort, (residual - mean) * per_count, 0.0)
            odds = jnp.where(period < cohort, jnp.exp(both[0:8, span]), 0.0)
            product = odds * residual
            odds_sum = odds_sum + odds
            product_sum = product_sum + product
            treated_out[:, place] = treated[0:1]
            product_out[:, place] = product[0:1]
            odds_out[:, place] = odds[0:1]
            pairs = []
            for value in (treated, product, odds):
                high = value.astype(BF16).astype(F32)
                pairs.append(jnp.concatenate([high, value - high], axis=0).astype(BF16))
            parts.append(jnp.concatenate(pairs, axis=0))
        total = total + jnp.dot(
            jnp.concatenate(parts, axis=1), mult[chunk_of(i), :], preferred_element_type=F32
        )
    col = iota((8, WIDTH), 1)
    both = jnp.where(
        col == 0,
        jnp.sum(odds_sum, axis=1, keepdims=True),
        jnp.where(col == 1, jnp.sum(product_sum, axis=1, keepdims=True), 0.0),
    )
    rows = [(total[16 * s : 16 * s + 8] + total[16 * s + 8 : 16 * s + 16])[0:4] for s in range(3)]
    rows = jnp.concatenate(rows + [both[0:4]], axis=0)
    for p in range(out.shape[0]):
        out[p] = rows


def relay_kernel(arrived, out):
    total = summed(arrived)[:, : out.shape[2]]
    for p in range(out.shape[0]):
        out[p] = total


def finish_kernel(total_rows, arrived, treated, product, odds, influence, bootstrap):
    cell = lax.axis_index("cell")
    sums = summed(arrived)
    weight = lane(sums[12:16], 0)
    mean = lane(sums[12:16], 1) / weight
    draws = math.sqrt(total_rows) * (sums[0:4] - (sums[4:8] - mean * sums[8:12]) / weight)
    for slot in range(4):
        bootstrap[pl.ds(cell ^ slot, 1), :] = draws[slot : slot + 1]
    scale = total_rows / weight[0:1, 0:1]
    influence[...] = total_rows * treated[...] - scale * (product[...] - mean[0:1, 0:1] * odds[...])


def swap_cores(value):
    return lax.ppermute(value, "core", [(0, 1), (1, 0)])


def to_pairs(payload):
    return lax.all_to_all(payload, ("y", "core"), 0, 0)


def to_line(arrived, size):
    peers = lax.axis_size("z")
    copies = call(relay_kernel, "relay", [shape(peers, arrived.shape[1], size)], [VMEM])(arrived)
    return lax.all_to_all(copies[0], "z", 0, 0)


def call(kernel, name, outs, ins, out_specs=None, scratch=(), cost=None):
    return pl.pallas_call(
        kernel,
        out_shape=outs,
        in_specs=ins,
        out_specs=out_specs or [VMEM] * len(outs),
        scratch_shapes=list(scratch),
        compiler_params=PARAMS,
        cost_estimate=cost,
        name=name,
    )


def shards(covariates, outcomes, multipliers, cohorts, cells):
    rows_here = covariates.shape[0]
    total_rows = rows_here * lax.axis_size(ROWS)
    pairs = lax.axis_size(("y", "core"))
    sems = pltpu.SemaphoreType.DMA((rows_here // CHUNK,))
    vector = shape(1, rows_here)
    eight = shape(8, WIDTH)
    cost = pl.CostEstimate(flops=1 << 33, bytes_accessed=10 << 20, transcendentals=0)
    tall, wide, payload = call(
        first_kernel,
        "first",
        [
            shape(rows_here, WIDTH, dtype=BF16),
            shape(WIDTH, rows_here, dtype=BF16),
            shape(pairs, 2, 17 * WIDTH),
        ],
        [HBM] * 4,
        [FREE, FREE, VMEM],
        [
            pltpu.SMEM(cells.shape, jnp.int32),
            pltpu.SMEM(cohorts.shape, jnp.int32),
            pltpu.VMEM(outcomes.shape, F32),
            sems,
            sems,
            pltpu.SemaphoreType.DMA((2,)),
        ],
    )(*(pltpu.with_memory_space_constraint(v, pltpu.HBM) for v in (cells, cohorts, covariates, outcomes)))
    halfway = to_pairs(payload)
    arrived = to_line(halfway, 17 * WIDTH)
    control = call(
        control_kernel, "control", [shape(72, WIDTH)], [SMEM, SMEM, FREE, FREE, FREE], cost=cost
    )(cells, cohorts, tall, wide, outcomes)[0]
    coefs = jnp.zeros((8, WIDTH), F32)
    kept = []
    for step in range(2):
        coefs, keep, payload = call(
            functools.partial(newton_kernel, step == 0),
            "newton",
            [eight, eight, shape(pairs, 2, 22 * WIDTH)],
            [SMEM, SMEM, VMEM, VMEM, FREE, FREE, VMEM, VMEM],
        )(cells, cohorts, arrived, swap_cores(arrived), tall, wide, coefs, control)
        kept.append(keep)
        halfway = to_pairs(payload)
        arrived = to_line(halfway, (22 - 5 * step) * WIDTH)
    ols = call(control_solve_kernel, "ols", [eight], [VMEM, VMEM], cost=cost)(halfway, kept[1])[0]
    arrived, ols = lax.optimization_barrier((arrived, ols))
    message = call(last_kernel, "last", [eight], [SMEM] + [VMEM] * 5)(
        cells, arrived, swap_cores(arrived), ols, coefs, kept[0]
    )[0]
    near, deep, mult = call(
        bring_kernel,
        "bring",
        [shape(rows_here, WIDTH, dtype=BF16), shape(*outcomes.shape), shape(rows_here, WIDTH, dtype=BF16)],
        [VMEM] + [HBM] * 3,
        [FREE] * 3,
        [sems, sems, sems],
        cost,
    )(
        message,
        *(pltpu.with_memory_space_constraint(v, pltpu.HBM) for v in (covariates, outcomes, multipliers)),
    )
    messages = [message] + [
        lax.ppermute(message, "cell", [(i, i ^ s) for i in range(4)]) for s in range(1, 4)
    ]
    payload, treated, product, odds = call(
        draws_kernel,
        "draws",
        [shape(pairs, 16, WIDTH), vector, vector, vector],
        [SMEM] + [VMEM] * 4 + [FREE] * 3,
    )(cohorts, *messages, near, deep, mult)
    arrived = to_line(to_pairs(payload), WIDTH)
    return call(
        functools.partial(finish_kernel, total_rows),
        "finish",
        [vector, shape(4, WIDTH)],
        [VMEM] * 4,
    )(arrived, treated, product, odds)


def solution(mesh):
    fine = Mesh(mesh.devices.reshape(4, 8, 2, 4), ROWS + ("cell",))
    return jax.shard_map(
        shards,
        mesh=fine,
        in_specs=(P(ROWS, None), P(None, ROWS), P(ROWS, "cell"), P(ROWS), P("cell", None)),
        out_specs=(P("cell", ROWS), P(None, "cell")),
        check_vma=False,
    )
```

```python
import functools
import math

import jax
import jax.numpy as jnp
from jax import lax
from jax.experimental import pallas as pl
from jax.experimental.pallas import tpu as pltpu
from jax.sharding import Mesh, PartitionSpec as P

ROWS = ("y", "z", "core")
F32 = jnp.float32
BF16 = jnp.bfloat16
WIDTH = 128
HALF = 64
CHUNK = 4096
VMEM = pl.BlockSpec(memory_space=pltpu.VMEM)
SMEM = pl.BlockSpec(memory_space=pltpu.SMEM)
HBM = pl.BlockSpec(memory_space=pltpu.HBM)
FREE = pl.BlockSpec()
PARAMS = pltpu.CompilerParams(vmem_limit_bytes=24 << 20)


def shape(*dims, dtype=F32):
    return jax.ShapeDtypeStruct(dims, dtype)


def iota(dims, axis):
    return lax.broadcasted_iota(jnp.int32, dims, axis)


def fold(gram):
    top, low = gram[:HALF], gram[HALF:]
    row, col = iota((HALF, WIDTH), 0), iota((HALF, WIDTH), 1)
    folded = jnp.where((col < HALF) & (col > row), pltpu.roll(low, HALF, 1), top)
    diagonal = jnp.sum(jnp.where(col - HALF == row, low, 0.0), axis=0, keepdims=True)
    return folded, diagonal


def unfold(folded, diagonal):
    row, col = iota((HALF, WIDTH), 0), iota((HALF, WIDTH), 1)
    turned = jnp.concatenate([folded, jnp.zeros_like(folded)], axis=0).T
    top = jnp.where((col >= HALF) | (col <= row), folded, turned[:HALF])
    right = col - HALF
    low = jnp.where(
        right > row,
        pltpu.roll(folded, HALF, 1),
        jnp.where(right < row, pltpu.roll(turned[:HALF], HALF, 1), diagonal),
    )
    return top, jnp.where(col < HALF, turned[HALF:], low)


def packed(rows):
    spots = [(i, i + 17) for i in range(17)] + [(i, i + 5) for i in range(34, rows.shape[0] - 5)]
    return jnp.concatenate(
        [jnp.concatenate([rows[i : i + 1], rows[j : j + 1]], axis=0) for i, j in spots], axis=1
    )


def unpacked(value, first, count):
    rows = []
    for i in range(first, first + count):
        part, spot = divmod(i, 17) if i < 34 else divmod(i - 34, 5)
        spot = spot + 17 if i >= 34 else spot
        rows.append(value[part : part + 1, spot * WIDTH : (spot + 1) * WIDTH])
    return jnp.concatenate(rows, axis=0)


def write_payload(out, folded, extras, more=None):
    for p in range(out.shape[0]):
        h = p % 2
        rows = [folded[32 * h : 32 * h + 32], extras[h], jnp.zeros((1, WIDTH), F32)]
        rows += [more[p]] if more else []
        out[p] = packed(jnp.concatenate(rows, axis=0))


def summed(ref):
    total = ref[0]
    for p in range(1, ref.shape[0]):
        total = total + ref[p]
    return total


def lane(block, i):
    return jnp.broadcast_to(block[:, i : i + 1], block.shape)


def sub(block, i):
    return jnp.broadcast_to(block[i : i + 1, :], block.shape)


def tree(terms):
    while len(terms) > 1:
        terms = [terms[i] + terms[i + 1] for i in range(0, len(terms), 2)]
    return terms[0]


def solve(top, low, vector):
    blocks = [top[8 * i : 8 * i + 8] for i in range(8)] + [low[8 * i : 8 * i + 8] for i in range(8)]
    blocks.append(jnp.broadcast_to(vector, (8, WIDTH)))
    row = iota((8, WIDTH), 0)
    columns = [lane(blocks[0], m) for m in range(8)]
    for k in range(16):
        col = iota((8, WIDTH), 1) - 8 * k
        inside = (col >= 0) & (col < 8)
        scaled = jnp.where(inside, jnp.where(col == row, 1.0, 0.0), blocks[k])
        ahead = [lane(blocks[k], 8 * k + 8 + m) for m in range(8)] if k < 15 else []
        for j in range(0, 8, 2):
            left, right = columns[j], columns[j + 1]
            a, b, d = sub(left, j), sub(right, j), sub(right, j + 1)
            scale = 1.0 / (a * d - b * b)
            a, b, d = a * scale, b * scale, d * scale
            here, there = row == j, row == j + 1
            pair = here | there
            first = jnp.where(here, -d, jnp.where(there, b, left * d - right * b))
            second = jnp.where(here, b, jnp.where(there, -a, right * a - left * b))

            def step(block):
                return jnp.where(pair, 0.0, block) - first * sub(block, j) - second * sub(block, j + 1)

            for m in range(j + 2, 8):
                columns[m] = step(columns[m])
            ahead = [step(block) for block in ahead]
            scaled = step(scaled)
        if k < 15:
            factors = [lane(blocks[k + 1], 8 * k + j) for j in range(8)]
            columns = [
                lane(blocks[k + 1], 8 * k + 8 + m)
                - tree([factors[j] * sub(ahead[m], j) for j in range(8)])
                for m in range(8)
            ]
        rows = [sub(scaled, j) for j in range(8)]
        for i in range(k + 1, 17):
            change = lane(blocks[i], 8 * k) * rows[0]
            for j in range(1, 8):
                change = change + lane(blocks[i], 8 * k + j) * rows[j]
            blocks[i] = jnp.where(inside, change, blocks[i] - change)
    return blocks[16]


def halves(core, own, other):
    is_first = core == 0
    first = jnp.where(is_first, own, other)
    second = jnp.where(is_first, other, own)
    folded = jnp.concatenate([first[:32], second[:32]], axis=0)
    return folded, first[32:33], second[32:33]


def arrivals(source, target, sems, axis):
    copies = []
    for i in range(target.shape[axis] // CHUNK):
        span = pl.ds(i * CHUNK, CHUNK)
        place = (span, slice(None)) if axis == 0 else (slice(None), span)
        copies.append(pltpu.make_async_copy(source.at[place], target.at[place], sems.at[i]))
        copies[-1].start()
    return copies


def chunk_of(i):
    return slice(i * CHUNK, (i + 1) * CHUNK)


def flag(condition, dtype=F32):
    return jnp.where(condition, 1.0, 0.0).astype(dtype)


def first_kernel(
    cells_hbm, cohorts_hbm, x_hbm, y_hbm, x, xt, out, cells, cohorts, y, x_sems, y_sems, sems
):
    per = CHUNK // WIDTH
    small = [
        pltpu.make_async_copy(cells_hbm, cells, sems.at[0]),
        pltpu.make_async_copy(cohorts_hbm, cohorts, sems.at[1]),
    ]
    for copy in small:
        copy.start()
    x_copies = arrivals(x_hbm, x, x_sems, 0)
    y_copies = arrivals(y_hbm, y, y_sems, 1)
    for copy in small:
        copy.wait()
    group, period = cells[0, 0], cells[0, 1]
    total = jnp.zeros((WIDTH + 16, WIDTH), F32)
    changes = jnp.zeros((1, WIDTH), F32)
    for i, copy in enumerate(x_copies):
        copy.wait()
        here = x[chunk_of(i), :]
        turned = here.T
        xt[:, chunk_of(i)] = turned
        left, marks = [], []
        for b in range(per):
            cohort = cohorts[i * per + b]
            treated = flag(cohort == group)
            eligible = treated + flag(cohort > period)
            left.append(turned[:, b * WIDTH : (b + 1) * WIDTH] * eligible.astype(BF16))
            marks.append(jnp.full((16, WIDTH), treated, F32).astype(BF16))
        left = jnp.concatenate([jnp.concatenate(left, axis=1), jnp.concatenate(marks, axis=1)], axis=0)
        total = total + jnp.dot(left, here, preferred_element_type=F32)
    for copy in y_copies:
        copy.wait()
    change = y[pl.ds(period, 1), :] - y[pl.ds(group - 1, 1), :]
    for b in range(cohorts.shape[0]):
        changes = changes + flag(cohorts[b] == group) * change[:, b * WIDTH : (b + 1) * WIDTH]
    folded, diagonal = fold(total[:WIDTH])
    scalar = jnp.sum(changes, axis=1, keepdims=True)
    first_lane = iota((1, WIDTH), 1) == 0
    write_payload(out, folded, (total[WIDTH : WIDTH + 1], jnp.where(first_lane, scalar, diagonal)))


def control_rows(group, period, cohorts, x, xt, y):
    per = CHUNK // WIDTH
    total = jnp.zeros((WIDTH + 16, WIDTH), F32)
    for i in range(x.shape[0] // CHUNK):
        span = pl.ds(i * CHUNK, CHUNK)
        change = y[pl.ds(period, 1), span] - y[pl.ds(group - 1, 1), span]
        change = jnp.broadcast_to(change, (16, CHUNK)).astype(BF16)
        turned = jnp.concatenate([xt[:, chunk_of(i)], change], axis=0)
        left = []
        for b in range(per):
            control = flag(cohorts[i * per + b] > period).astype(BF16)
            left.append(turned[:, b * WIDTH : (b + 1) * WIDTH] * control)
        left = jnp.concatenate(left, axis=1)
        total = total + jnp.dot(left, x[chunk_of(i), :], preferred_element_type=F32)
    folded, diagonal = fold(total[:WIDTH])
    return folded, jnp.concatenate([total[WIDTH : WIDTH + 1], diagonal], axis=0)


def newton_kernel(
    first, cells, cohorts, own, other, x, xt, before, y, coefs, keep, out
):
    group, period = cells[0, 0], cells[0, 1]
    per = CHUNK // WIDTH
    if first:
        control, ends = control_rows(group, period, cohorts, x, xt, y)
    mine = summed(own)
    core = lax.axis_index("core")
    folded, row, diagonal = halves(core, unpacked(mine, 0, 33), unpacked(summed(other), 0, 33))
    top, low = unfold(folded, diagonal)
    if first:
        keep[...] = jnp.concatenate([row, diagonal, jnp.zeros((6, WIDTH), F32)], axis=0)
        new = 4.0 * solve(top, low, row - 0.5 * top[0:1])
    else:
        keep[...] = jnp.concatenate([unpacked(mine, 34, 2), jnp.zeros((6, WIDTH), F32)], axis=0)
        new = before[...] + solve(top, low, row)
    coefs[...] = new
    rounded = jnp.concatenate([new, new], axis=0).astype(BF16)
    total = jnp.zeros((WIDTH + 16, WIDTH), F32)
    for i in range(x.shape[0] // CHUNK):
        turned = xt[:, chunk_of(i)]
        index = jnp.dot(rounded, turned, preferred_element_type=F32)[0:8]
        probability = jax.nn.sigmoid(index)
        weight = probability * (1.0 - probability)
        left, errors = [], []
        for b in range(per):
            cohort = cohorts[i * per + b]
            treated = flag(cohort == group)
            eligible = treated + flag(cohort > period)
            span = slice(b * WIDTH, (b + 1) * WIDTH)
            here = jnp.broadcast_to(weight[0:1, span] * eligible, (WIDTH, WIDTH))
            left.append((here * turned[:, span].astype(F32)).astype(BF16))
            error = (treated - probability[:, span]) * eligible
            errors.append(jnp.concatenate([error, error], axis=0).astype(BF16))
        left = jnp.concatenate([jnp.concatenate(left, axis=1), jnp.concatenate(errors, axis=1)], axis=0)
        total = total + jnp.dot(left, x[chunk_of(i), :], preferred_element_type=F32)
    folded, diagonal = fold(total[:WIDTH])
    if first:
        more = [
            jnp.concatenate([ends, control[8 * p : 8 * p + 8]], axis=0)
            for p in range(out.shape[0])
        ]
    else:
        piece = jnp.concatenate([jnp.zeros((2, WIDTH), F32), unpacked(mine, 36, 8)], axis=0)
        more = [piece] * out.shape[0]
    write_payload(out, folded, (total[WIDTH : WIDTH + 1], diagonal), more)


def control_solve_kernel(arrived, extras, out):
    folded = jnp.concatenate([unpacked(arrived[p], 36, 8) for p in range(arrived.shape[0])], axis=0)
    solved = solve(*unfold(folded, extras[1:2, :]), extras[0:1, :])
    out[...] = solved.astype(BF16).astype(F32)


def last_kernel(cells, own, other, control, before, keep, out):
    core = lax.axis_index("core")
    folded, row, diagonal = halves(core, unpacked(summed(own), 0, 33), unpacked(summed(other), 0, 33))
    new = before[...] + solve(*unfold(folded, diagonal), row)
    ols = control[0:1, :]
    treated_x = keep[0:1, :]
    count = lane(treated_x, 0)
    fitted = jnp.sum(ols * treated_x, axis=1, keepdims=True)
    mean = (lane(keep[1:2, :], 0) - fitted) / count
    out[...] = jnp.concatenate(
        [
            new[0:1].astype(BF16).astype(F32),
            ols,
            mean,
            count,
            jnp.full((1, WIDTH), cells[0, 0].astype(F32), F32),
            jnp.full((1, WIDTH), cells[0, 1].astype(F32), F32),
            jnp.zeros((2, WIDTH), F32),
        ],
        axis=0,
    )


def bring_kernel(message, x_hbm, y_hbm, mult_hbm, x, y, mult, x_sems, y_sems, mult_sems):
    copies = arrivals(x_hbm, x, x_sems, 0) + arrivals(y_hbm, y, y_sems, 1)
    for copy in copies + arrivals(mult_hbm, mult, mult_sems, 0):
        copy.wait()


def draws_kernel(
    cohorts, m0, m1, m2, m3, x, y, mult, out, treated_out, product_out, odds_out
):
    per = CHUNK // WIDTH
    blank = jnp.zeros((4, WIDTH), F32)

    def stacked(i):
        return jnp.concatenate([m[i : i + 1, :] for m in (m0, m1, m2, m3)] + [blank], axis=0)

    left = jnp.concatenate([stacked(0), stacked(1)], axis=0).astype(BF16)
    mean, count, group, period = stacked(2), stacked(3), stacked(4), stacked(5)
    valid = iota((8, WIDTH), 0) < 4
    per_count = jnp.where(valid, 1.0 / jnp.where(valid, count, 1.0), 0.0)
    group = jnp.where(valid, group, -1.0)
    period = jnp.where(valid, period, 99.0)
    signs = [flag(period == p) - flag(group - 1.0 == p) for p in range(8)]
    total = jnp.zeros((48, WIDTH), F32)
    odds_sum = jnp.zeros((8, WIDTH), F32)
    product_sum = jnp.zeros((8, WIDTH), F32)
    for i in range(x.shape[0] // CHUNK):
        both = lax.dot_general(
            left, x[chunk_of(i), :], (((1,), (1,)), ((), ())), preferred_element_type=F32
        )
        parts = []
        for b in range(per):
            span = slice(b * WIDTH, (b + 1) * WIDTH)
            place = slice(i * CHUNK + b * WIDTH, i * CHUNK + (b + 1) * WIDTH)
            cohort = cohorts[i * per + b].astype(F32)
            outcome = y[:, place]
            change = signs[0] * sub(outcome, 0)
            for p in range(1, 8):
                change = change + signs[p] * sub(outcome, p)
            residual = change - both[8:16, span]
            treated = jnp.where(group == cohort, (residual - mean) * per_count, 0.0)
            odds = jnp.where(period < cohort, jnp.exp(both[0:8, span]), 0.0)
            product = odds * residual
            odds_sum = odds_sum + odds
            product_sum = product_sum + product
            treated_out[:, place] = treated[0:1]
            product_out[:, place] = product[0:1]
            odds_out[:, place] = odds[0:1]
            pairs = []
            for value in (treated, product, odds):
                high = value.astype(BF16).astype(F32)
                pairs.append(jnp.concatenate([high, value - high], axis=0).astype(BF16))
            parts.append(jnp.concatenate(pairs, axis=0))
        total = total + jnp.dot(
            jnp.concatenate(parts, axis=1), mult[chunk_of(i), :], preferred_element_type=F32
        )
    col = iota((8, WIDTH), 1)
    both = jnp.where(
        col == 0,
        jnp.sum(odds_sum, axis=1, keepdims=True),
        jnp.where(col == 1, jnp.sum(product_sum, axis=1, keepdims=True), 0.0),
    )
    rows = [(total[16 * s : 16 * s + 8] + total[16 * s + 8 : 16 * s + 16])[0:4] for s in range(3)]
    rows = jnp.concatenate(rows + [both[0:4]], axis=0)
    for p in range(out.shape[0]):
        out[p] = rows


def relay_kernel(arrived, out):
    total = summed(arrived)[:, : out.shape[2]]
    for p in range(out.shape[0]):
        out[p] = total


def finish_kernel(total_rows, arrived, treated, product, odds, influence, bootstrap):
    cell = lax.axis_index("cell")
    sums = summed(arrived)
    weight = lane(sums[12:16], 0)
    mean = lane(sums[12:16], 1) / weight
    draws = math.sqrt(total_rows) * (sums[0:4] - (sums[4:8] - mean * sums[8:12]) / weight)
    for slot in range(4):
        bootstrap[pl.ds(cell ^ slot, 1), :] = draws[slot : slot + 1]
    scale = total_rows / weight[0:1, 0:1]
    influence[...] = total_rows * treated[...] - scale * (product[...] - mean[0:1, 0:1] * odds[...])


def swap_cores(value):
    return lax.ppermute(value, "core", [(0, 1), (1, 0)])


def to_pairs(payload):
    return lax.all_to_all(payload, ("y", "core"), 0, 0)


def to_line(arrived, size):
    peers = lax.axis_size("z")
    copies = call(relay_kernel, "relay", [shape(peers, arrived.shape[1], size)], [VMEM])(arrived)
    return lax.all_to_all(copies[0], "z", 0, 0)


def call(kernel, name, outs, ins, out_specs=None, scratch=(), cost=None):
    return pl.pallas_call(
        kernel,
        out_shape=outs,
        in_specs=ins,
        out_specs=out_specs or [VMEM] * len(outs),
        scratch_shapes=list(scratch),
        compiler_params=PARAMS,
        cost_estimate=cost,
        name=name,
    )


def shards(covariates, outcomes, multipliers, cohorts, cells):
    rows_here = covariates.shape[0]
    total_rows = rows_here * lax.axis_size(ROWS)
    pairs = lax.axis_size(("y", "core"))
    sems = pltpu.SemaphoreType.DMA((rows_here // CHUNK,))
    vector = shape(1, rows_here)
    eight = shape(8, WIDTH)
    cost = pl.CostEstimate(flops=1 << 33, bytes_accessed=10 << 20, transcendentals=0)
    tall, wide, payload = call(
        first_kernel,
        "first",
        [
            shape(rows_here, WIDTH, dtype=BF16),
            shape(WIDTH, rows_here, dtype=BF16),
            shape(pairs, 2, 17 * WIDTH),
        ],
        [HBM] * 4,
        [FREE, FREE, VMEM],
        [
            pltpu.SMEM(cells.shape, jnp.int32),
            pltpu.SMEM(cohorts.shape, jnp.int32),
            pltpu.VMEM(outcomes.shape, F32),
            sems,
            sems,
            pltpu.SemaphoreType.DMA((2,)),
        ],
    )(*(pltpu.with_memory_space_constraint(v, pltpu.HBM) for v in (cells, cohorts, covariates, outcomes)))
    halfway = to_pairs(payload)
    arrived = to_line(halfway, 17 * WIDTH)
    coefs = jnp.zeros((8, WIDTH), F32)
    kept = []
    for step in range(2):
        coefs, keep, payload = call(
            functools.partial(newton_kernel, step == 0),
            "newton",
            [eight, eight, shape(pairs, 2, 22 * WIDTH)],
            [SMEM, SMEM, VMEM, VMEM, FREE, FREE, VMEM, FREE],
        )(cells, cohorts, arrived, swap_cores(arrived), tall, wide, coefs, outcomes)
        kept.append(keep)
        halfway = to_pairs(payload)
        arrived = to_line(halfway, (22 - 5 * step) * WIDTH)
    ols = call(control_solve_kernel, "ols", [eight], [VMEM, VMEM], cost=cost)(halfway, kept[1])[0]
    arrived, ols = lax.optimization_barrier((arrived, ols))
    message = call(last_kernel, "last", [eight], [SMEM] + [VMEM] * 5)(
        cells, arrived, swap_cores(arrived), ols, coefs, kept[0]
    )[0]
    near, deep, mult = call(
        bring_kernel,
        "bring",
        [shape(rows_here, WIDTH, dtype=BF16), shape(*outcomes.shape), shape(rows_here, WIDTH, dtype=BF16)],
        [VMEM] + [HBM] * 3,
        [FREE] * 3,
        [sems, sems, sems],
        cost,
    )(
        message,
        *(pltpu.with_memory_space_constraint(v, pltpu.HBM) for v in (covariates, outcomes, multipliers)),
    )
    messages = [message] + [
        lax.ppermute(message, "cell", [(i, i ^ s) for i in range(4)]) for s in range(1, 4)
    ]
    payload, treated, product, odds = call(
        draws_kernel,
        "draws",
        [shape(pairs, 16, WIDTH), vector, vector, vector],
        [SMEM] + [VMEM] * 4 + [FREE] * 3,
    )(cohorts, *messages, near, deep, mult)
    arrived = to_line(to_pairs(payload), WIDTH)
    return call(
        functools.partial(finish_kernel, total_rows),
        "finish",
        [vector, shape(4, WIDTH)],
        [VMEM] * 4,
    )(arrived, treated, product, odds)


def solution(mesh):
    fine = Mesh(mesh.devices.reshape(4, 8, 2, 4), ROWS + ("cell",))
    return jax.shard_map(
        shards,
        mesh=fine,
        in_specs=(P(ROWS, None), P(None, ROWS), P(ROWS, "cell"), P(ROWS), P("cell", None)),
        out_specs=(P("cell", ROWS), P(None, "cell")),
        check_vma=False,
    )
```
